128 devices in a mesh: wave: 16 (over x_lo, z, core), lev: 8 (over x_hi, y).
Axes of the slice: x: 4 (x_hi: 2, x_lo: 2; x = x_hi * 2 + x_lo), y: 4, z: 4, core: 2. Of those that a mesh axis runs over, the one named last changes fastest.
Arguments:
- grid_in: float32 [1, 136, 640, 1280], P(None, 'lev', 'wave'), may hold values from -6 to 6
- wavenumbers: int32 [384], replicated, may hold values from 0 to 383, each once
- legendre: float32 [384, 640, 640], P(('wave', 'lev')), may hold values from -0.25 to 0.25
- modes_in: float32 [136, 136], replicated, may hold values from -0.5 to 0.5
- modes_out: float32 [136, 136], replicated, may hold values from -0.5 to 0.5
- damping: float32 [136], replicated, may hold values from 7.347161e-07 to 7.347161e-05
Outputs:
- grid_out: float32 [1, 136, 640, 1280], P(None, 'lev', 'wave')
The draws below stay inside these ranges and needn't reach their ends.
Inputs may be any that keep to these rules, and one draw needn't show every extreme that they name: `wavenumbers`: each of 0 to 383 stands once; slot s lies on the device of index s // 3 in the joined wave+lev order.
All inputs are finite; a program needn't handle non-finite values.
Results may differ from the reference program's by a relative error of at most 0.0003.
Values sent between devices are 32-bit elements; how exact they have to be, the bound alone decides.
A program may use at most 128 MiB of HBM per device.

```python
import math
import jax
import jax.numpy as jnp
from jax import lax

NLON = 1280
NLAT = 640
K = 136
MW = 384
FIELDS = 1
NN = 640


def shard_levels(own_key, dims, shards, least, top_value):
    def one(axis_at, parts):
        draws = jax.random.uniform(jax.random.fold_in(jax.random.fold_in(own_key, 6), axis_at), (parts,), jnp.float32, least / len(shards), top_value / len(shards))
        return jnp.repeat(jnp.exp(draws), dims[axis_at] // parts).reshape((-1,) + (1,) * (len(dims) - axis_at - 1))

    level = one(*shards[0])
    for cut in shards[1:]:
        level = level * one(*cut)
    return level


def centred(key, extent, deviation, most, split=(), held_as=jnp.bfloat16):
    level = shard_levels(key, extent, split, -0.22, 0.18) if split else 1.0
    entries = jax.random.normal(key, extent, jnp.float32) * deviation * level
    return jnp.minimum(jnp.maximum(entries, -most), most).astype(held_as)


def setup_inputs(seed: int = 0) -> dict:
    splits = jax.random.split(jax.random.key(seed), 7)
    grid_in = centred(splits[0], (FIELDS, K, NLAT, NLON), 1.0, 6.0, ((1, 8), (2, 16)), jnp.float32)
    wavenumbers = jax.random.permutation(splits[1], MW).astype(jnp.int32)
    legendre = centred(splits[2], (MW, NLAT, NN), NLAT ** -0.5, 0.25, ((0, 128),), jnp.float32)
    modes_in = centred(splits[3], (K, K), K ** -0.5, 0.5, (), jnp.float32)
    modes_out = centred(splits[4], (K, K), K ** -0.5, 0.5, (), jnp.float32)
    damping = jnp.clip(jnp.exp(jax.random.uniform(splits[5], (K,), jnp.float32, math.log(7.347160817516851e-07), math.log(7.347160862991586e-05))), 7.347160817516851e-07, 7.347160862991586e-05)
    return dict(grid_in=grid_in, wavenumbers=wavenumbers, legendre=legendre, modes_in=modes_in, modes_out=modes_out, damping=damping)


two_pi = 2.0 * math.pi
highest = lax.Precision.HIGHEST

def dft_table(wavenumbers, lon_count):
    longitude = jnp.arange(lon_count, dtype=jnp.int32)
    phase = wavenumbers.astype(jnp.int32)[:, None] * longitude[None, :] % lon_count
    angle = phase.astype(jnp.float32) * (two_pi / lon_count)
    scale = 1.0 / math.sqrt(lon_count)
    table = jnp.stack([jnp.cos(angle), -jnp.sin(angle)], axis=1) * scale
    return table.reshape(2 * wavenumbers.shape[0], lon_count)

def reference(grid_in, wavenumbers, legendre, modes_in, modes_out, damping):
    fields, levels, lat_count, lon_count = grid_in.shape
    slot_count = wavenumbers.shape[0]
    coeff_count = legendre.shape[2]
    lon_table = dft_table(wavenumbers, lon_count)
    fourier = jnp.einsum('rx,fklx->rfkl', lon_table, grid_in, precision=highest)
    fourier = fourier.reshape(slot_count, 2, fields, levels, lat_count)

    def per_slot(packed):
        columns, plm, wave = packed
        spectral = jnp.einsum('cfkl,lj->cfkj', columns, plm, precision=highest)
        degree = wave + jnp.arange(coeff_count, dtype=jnp.int32)
        inside = degree <= coeff_count - 1
        spectral = jnp.where(inside[None, None, None, :], spectral, jnp.float32(0.0))
        growth = (degree * (degree + 1)).astype(jnp.float32)
        factor = 1.0 / (1.0 + damping[:, None] * growth[None, :])
        modal = jnp.einsum('qk,cfkj->cfqj', modes_in, spectral, precision=highest) * factor[None, None, :, :]
        solved = jnp.einsum('kq,cfqj->cfkj', modes_out, modal, precision=highest)
        return jnp.einsum('lj,cfkj->cfkl', plm, solved, precision=highest)
    returned = lax.map(per_slot, (fourier, legendre, wavenumbers.astype(jnp.int32)))
    returned = returned.reshape(2 * slot_count, fields, levels, lat_count)
    return jnp.einsum('rx,rfkl->fklx', lon_table, returned, precision=highest)
```

```python
import math

import jax
import jax.numpy as jnp
from jax import lax
from jax.experimental import pallas as pl
from jax.experimental.pallas import tpu as pltpu
from jax.sharding import PartitionSpec as P

MESH = pl.DeviceIdType.MESH
f32 = jnp.float32
bf16 = jnp.bfloat16

LON = 1280
LAT = 640
COEFF = 640
WAVES = 16
LEVS = 8
DEVS = WAVES * LEVS
LV = 17
LT = 40
SLOTS = 3
LEVELS = LEVS * LV
PAD = 144
ROWS = 16
HALF = DEVS * ROWS
MAIN = 16 * LT // 128


def split(x):
    hi = x.astype(bf16)
    return hi, (x - hi.astype(f32)).astype(bf16)


def dot(a, b, dims):
    return lax.dot_general(a, b, (dims, ((), ())), preferred_element_type=f32)


NN = ((1,), (0,))
NT = ((1,), (1,))


def dot3(ah, al, bh, bl, dims):
    return dot(ah, bh, dims) + dot(al, bh, dims) + dot(ah, bl, dims)


def lanes(rows):
    return lax.broadcasted_iota(jnp.int32, (rows, 128), 1)


def pick(tile, get):
    lane = lanes(8)
    value = None
    for p in range(128 * tile // LT, (128 * tile + 127) // LT + 1):
        value = get(p) if value is None else jnp.where(lane < LT * p - 128 * tile, value, get(p))
    return value


def ring(tiles, shift):
    whole, part = divmod(shift % (128 * MAIN), 128)
    if part == 0:
        return [tiles[(t + whole) % MAIN] for t in range(MAIN)]
    lane = lanes(8)
    rolled = [pltpu.roll(x, 128 - part, 1) for x in tiles]
    return [
        jnp.where(lane < 128 - part, rolled[(t + whole) % MAIN], rolled[(t + whole + 1) % MAIN])
        for t in range(MAIN)
    ]


def kernel(
    waves, damp, modes_f32, cos1, sin1, cos2, sin2, grid, plm, out,
    gf, gh, gl, pf, ph, pw, th, tl, s1, r1, s2, r2, x, e, acc, rth, rtl, modes,
    load_sem, send1, recv1, send2, recv2,
):
    w = lax.axis_index("wave")
    v = lax.axis_index("lev")
    me = w * LEVS + v

    def peer(i):
        t = lax.rem(me + i, DEVS)
        return t, (t // LEVS, lax.rem(t, LEVS))

    for p in range(16):
        pltpu.make_async_copy(
            grid.at[lax.rem(p - w + 16, 16)], gf.at[pl.ds(LT * p, LT)], load_sem.at[0]
        ).start()
    for s in range(SLOTS):
        pltpu.make_async_copy(
            grid.at[16], gf.at[pl.ds(16 * LT + LT * s, LT)], load_sem.at[0]
        ).start()
    for s in range(SLOTS):
        pltpu.make_async_copy(plm.at[s], pf.at[pl.ds(LAT * s, LAT)], load_sem.at[1]).start()

    barrier = pltpu.get_barrier_semaphore()

    def greet(i, carry):
        pl.semaphore_signal(barrier, inc=1, device_id=peer(i)[1], device_id_type=MESH)
        return carry

    lax.fori_loop(1, DEVS, greet, 0)

    def table(i, carry):
        rows = pl.ds(pl.multiple_of(32 * i, 32), 32)
        rows_sin = pl.ds(pl.multiple_of(32 * i + 384, 32), 32)
        c1, n1 = cos1[rows, :], sin1[rows, :]
        c2, n2 = cos2[rows, :], sin2[rows, :]
        for a in range(LON // 128):
            ca, sa = c2[:, a : a + 1], n2[:, a : a + 1]
            col = slice(128 * a, 128 * a + 128)
            hi, lo = split(c1 * ca - n1 * sa)
            th[rows, col] = hi
            tl[rows, col] = lo
            hi, lo = split(-(n1 * ca + c1 * sa))
            th[rows_sin, col] = hi
            tl[rows_sin, col] = lo
        return carry

    lax.fori_loop(0, 12, table, 0)

    pltpu.make_async_copy(gf.at[pl.ds(0, 760)], gf.at[pl.ds(0, 760)], load_sem.at[0]).wait()
    gf[760:768, :] = jnp.zeros((8, LON), f32)

    def split_grid(i, carry):
        rows = pl.ds(pl.multiple_of(32 * i, 32), 32)
        gh[rows, :], gl[rows, :] = split(gf[rows, :])
        return carry

    lax.fori_loop(0, 24, split_grid, 0)

    lane128 = lanes(128)

    def forward_dft(c):
        def step(n, carry):
            cols = pl.ds(pl.multiple_of(256 * n, 256), 256)
            part = slice(384 * c, 384 * c + 384)
            y = dot3(th[part, :], tl[part, :], gh[cols, :], gl[cols, :], NT)
            for h in range(2):
                yh = y[:, 128 * h : 128 * h + 128]

                def main():
                    for s in range(SLOTS):
                        start = HALF * c + MAIN * s + 2 * n + h
                        s1[pl.ds(start, DEVS, ROWS), :] = yh[128 * s : 128 * s + 128]

                if h == 0:
                    main()
                else:
                    pl.when(n < 2)(main)

                    @pl.when(n == 2)
                    def _():
                        last = jnp.where(
                            lane128 < LT,
                            yh[0:128],
                            jnp.where(lane128 < 2 * LT, yh[128:256], yh[256:384]),
                        )
                        s1[pl.ds(HALF * c + ROWS - 1, DEVS, ROWS), :] = last

            return carry

        lax.fori_loop(0, 3, step, 0)

    def block(c, d):
        return pl.ds(pl.multiple_of((c * DEVS + d) * ROWS, ROWS), ROWS)

    def send(c, src, dst, send_sem, recv_sem):
        pltpu.make_async_copy(src.at[block(c, me)], dst.at[block(c, me)], recv_sem.at[c]).start()

        def go(i, carry):
            t, where = peer(i)
            pltpu.make_async_remote_copy(
                src_ref=src.at[block(c, t)],
                dst_ref=dst.at[block(c, me)],
                send_sem=send_sem.at[c],
                recv_sem=recv_sem.at[c],
                device_id=where,
                device_id_type=MESH,
            ).start()
            return carry

        lax.fori_loop(1, DEVS, go, 0)

    def arrive(c, dst, recv_sem):
        half = dst.at[pl.ds(HALF * c, HALF)]
        pltpu.make_async_copy(half, half, recv_sem.at[c]).wait()

    def sent(c, src, send_sem):
        part = src.at[pl.ds(0, HALF - ROWS)]
        pltpu.make_async_copy(part, part, send_sem.at[c]).wait()

    forward_dft(0)
    pl.semaphore_wait(barrier, DEVS - 1)
    send(0, s1, r1, send1, recv1)
    forward_dft(1)
    send(1, s1, r1, send1, recv1)

    pltpu.make_async_copy(pf, pf, load_sem.at[1]).wait()

    def split_plm(i, carry):
        rows = pl.ds(pl.multiple_of(64 * i, 64), 64)
        ph[rows, :], pw[rows, :] = split(pf[rows, :])
        return carry

    lax.fori_loop(0, SLOTS * LAT // 64, split_plm, 0)

    modes[0], modes[1] = split(modes_f32[0])
    modes[2], modes[3] = split(modes_f32[1])
    x[LEVELS:PAD, :] = jnp.zeros((PAD - LEVELS, LAT), f32)
    lane8 = lanes(8)

    def middle(c):
        acc[...] = jnp.zeros((WAVES * 8, 128), f32)

        def slot(s, carry):
            base = HALF * c + MAIN * s
            for k in range(16):
                tiles = [
                    pick(t, lambda p: r1[pl.ds(base + ((p - k) % 16) * 128 + t, 8, ROWS), :])
                    for t in range(MAIN)
                ]
                for t, value in enumerate(ring(tiles, LT * k)):
                    x[8 * k : 8 * k + 8, 128 * t : 128 * t + 128] = value
            tiles = [None] * MAIN
            for q in range(WAVES):
                own = r1[pl.ds(HALF * c + q * 128 + ROWS - 1, 8, ROWS), :]
                own = pltpu.roll(own, lax.rem(LT * q - LT * s + 768, 128), 1)
                t, off = divmod(LT * q, 128)
                tiles[t] = own if off == 0 else jnp.where(lane8 < off, tiles[t], own)
                if off + LT > 128:
                    tiles[t + 1] = own
            for t in range(MAIN):
                x[128:136, 128 * t : 128 * t + 128] = tiles[t]

            prow = pl.ds(pl.multiple_of(LAT * s, LAT), LAT)
            xh, xl = split(x[...])
            spec = dot3(xh, xl, ph[prow, :], pw[prow, :], NN)
            degree = waves[SLOTS * me + s] + lax.broadcasted_iota(jnp.int32, (PAD, COEFF), 1)
            growth = (degree * (degree + 1)).astype(f32)
            factor = jnp.where(degree < COEFF, 1.0 / (1.0 + damp[...] * growth), 0.0)
            sh, sl = split(spec)
            modal = dot3(modes[0], modes[1], sh, sl, NN) * factor
            mh, ml = split(modal)
            solved = dot3(modes[2], modes[3], mh, ml, NN)
            vh, vl = split(solved)
            x[...] = dot3(vh, vl, ph[prow, :], pw[prow, :], NT)

            for k in range(16):
                tiles = [x[8 * k : 8 * k + 8, 128 * t : 128 * t + 128] for t in range(MAIN)]
                for t, value in enumerate(ring(tiles, -LT * k)):
                    e[8 * k : 8 * k + 8, 128 * t : 128 * t + 128] = value
            for q in range(WAVES):
                for t in range(MAIN):

                    def get(p):
                        k = (p - q) % 16
                        return e[8 * k : 8 * k + 8, 128 * t : 128 * t + 128]

                    s2[pl.ds(base + q * 128 + t, 8, ROWS), :] = pick(t, get)
                t, off = divmod(LT * q, 128)
                own = x[128:136, 128 * t : 128 * t + 128]
                if off + LT > 128:
                    after = x[128:136, 128 * t + 128 : 128 * t + 256]
                    own = jnp.where(lane8 < off, after, own)
                own = pltpu.roll(own, lax.rem(LT * s - LT * q + 768, 128), 1)
                inside = (lane8 >= LT * s) & (lane8 < LT * s + LT)
                acc[8 * q : 8 * q + 8, :] = jnp.where(inside, own, acc[8 * q : 8 * q + 8, :])
            return carry

        lax.fori_loop(0, SLOTS, slot, 0)
        s2[pl.ds(HALF * c + ROWS - 1, DEVS, ROWS), :] = acc[...]

    for c in range(2):
        arrive(c, r1, recv1)
        middle(c)
        send(c, s2, r2, send2, recv2)

    def adjoint_dft(c):
        for s in range(SLOTS):
            for t in range(MAIN):
                tile = r2[pl.ds(HALF * c + MAIN * s + t, DEVS, ROWS), :]
                hi, lo = split(tile.T)
                rth[128 * t : 128 * t + 128, 128 * s : 128 * s + 128] = hi
                rtl[128 * t : 128 * t + 128, 128 * s : 128 * s + 128] = lo
            tile = r2[pl.ds(HALF * c + ROWS - 1, DEVS, ROWS), :]
            inside = (lane128 >= LT * s) & (lane128 < LT * s + LT)
            hi, lo = split(jnp.where(inside, tile, 0.0).T)
            rth[128 * MAIN :, 128 * s : 128 * s + 128] = hi
            rtl[128 * MAIN :, 128 * s : 128 * s + 128] = lo

        def step(n, carry):
            cols = pl.ds(pl.multiple_of(256 * n, 256), 256)
            part = slice(384 * c, 384 * c + 384)
            y = dot3(rth[...], rtl[...], th[part, cols], tl[part, cols], NN)
            if c == 0:
                gf[:, cols] = y
            else:
                gf[:, cols] += y
            return carry

        lax.fori_loop(0, LON // 256, step, 0)

    for c in range(2):
        arrive(c, r2, recv2)
        adjoint_dft(c)

    gf[640:680, :] = gf[640:680, :] + gf[680:720, :] + gf[720:760, :]
    for p in range(17):
        level = lax.rem(p - w + 16, 16) if p < 16 else 16
        pltpu.make_async_copy(gf.at[pl.ds(LT * p, LT)], out.at[level], load_sem.at[2]).start()
    for c in range(2):
        sent(c, s1, send1)
        sent(c, s2, send2)
    done = gf.at[pl.ds(0, 680)]
    pltpu.make_async_copy(done, done, load_sem.at[2]).wait()


def tables(wavenumbers):
    order = wavenumbers.reshape(DEVS, SLOTS).T.reshape(DEVS * SLOTS, 1)
    near = order * jnp.arange(128, dtype=jnp.int32)[None, :] % LON
    far = order * jnp.arange(16, dtype=jnp.int32)[None, :] % (LON // 128)
    near = near.astype(f32) * (2.0 * math.pi / LON)
    far = far.astype(f32) * (2.0 * math.pi / (LON // 128))
    scale = 1.0 / math.sqrt(LON)
    return jnp.cos(near) * scale, jnp.sin(near) * scale, jnp.cos(far), jnp.sin(far)


def local(grid_in, wavenumbers, legendre, modes_in, modes_out, damping):
    grid = grid_in.reshape(LV, LT, LON)
    m_in = modes_in.reshape(LEVELS, LEVS, LV).transpose(0, 2, 1).reshape(LEVELS, LEVELS)
    m_out = modes_out.reshape(LEVS, LV, LEVELS).transpose(1, 0, 2).reshape(LEVELS, LEVELS)
    pad = PAD - LEVELS
    modes = jnp.pad(jnp.stack([m_in, m_out]), ((0, 0), (0, pad), (0, pad)))
    damp = jnp.pad(damping, (0, pad)).reshape(PAD, 1)
    vmem = pl.BlockSpec(memory_space=pltpu.VMEM)
    hbm = pl.BlockSpec(memory_space=pl.ANY)
    dma = pltpu.SemaphoreType.DMA
    result = pl.pallas_call(
        kernel,
        out_shape=jax.ShapeDtypeStruct((LV, LT, LON), f32),
        in_specs=[pl.BlockSpec(memory_space=pltpu.SMEM)] + [vmem] * 6 + [hbm] * 2,
        out_specs=hbm,
        scratch_shapes=[
            pltpu.VMEM((768, LON), f32),
            pltpu.VMEM((768, LON), bf16),
            pltpu.VMEM((768, LON), bf16),
            pltpu.VMEM((SLOTS * LAT, COEFF), f32),
            pltpu.VMEM((SLOTS * LAT, COEFF), bf16),
            pltpu.VMEM((SLOTS * LAT, COEFF), bf16),
            pltpu.VMEM((768, LON), bf16),
            pltpu.VMEM((768, LON), bf16),
            pltpu.VMEM((2 * HALF, 128), f32),
            pltpu.VMEM((2 * HALF, 128), f32),
            pltpu.VMEM((2 * HALF, 128), f32),
            pltpu.VMEM((2 * HALF, 128), f32),
            pltpu.VMEM((PAD, LAT), f32),
            pltpu.VMEM((128, LAT), f32),
            pltpu.VMEM((WAVES * 8, 128), f32),
            pltpu.VMEM((768, 384), bf16),
            pltpu.VMEM((768, 384), bf16),
            pltpu.VMEM((4, PAD, PAD), bf16),
            dma((3,)),
            dma((2,)),
            dma((2,)),
            dma((2,)),
            dma((2,)),
        ],
        compiler_params=pltpu.CompilerParams(
            collective_id=0, has_side_effects=True, vmem_limit_bytes=56 << 20
        ),
        name="spectral_step",
    )(wavenumbers, damp, modes, *tables(wavenumbers), grid, legendre)
    return result.reshape(1, LV, LT, LON)


def solution(mesh):
    return jax.shard_map(
        local,
        mesh=mesh,
        in_specs=(P(None, "lev", "wave", None), P(), P(("wave", "lev"), None, None), P(), P(), P()),
        out_specs=P(None, "lev", "wave", None),
        check_vma=False,
    )
```

```python
import math

import jax
import jax.numpy as jnp
import numpy as np
from jax import lax
from jax.experimental import pallas as pl
from jax.experimental.pallas import tpu as pltpu
from jax.sharding import PartitionSpec as P

MESH = pl.DeviceIdType.MESH
f32 = jnp.float32
bf16 = jnp.bfloat16

LON = 1280
LAT = 640
COEFF = 640
WAVES = 16
LEVS = 8
DEVS = WAVES * LEVS
LV = 17
LT = 40
SLOTS = 3
LEVELS = LEVS * LV
PAD = 144
ROWS = 16
HALF = DEVS * ROWS
MAIN = 16 * LT // 128


def split(x):
    hi = x.astype(bf16)
    return hi, (x - hi.astype(f32)).astype(bf16)


def dot(a, b, dims):
    return lax.dot_general(a, b, (dims, ((), ())), preferred_element_type=f32)


TN = ((0,), (0,))
NN = ((1,), (0,))
NT = ((1,), (1,))


def dot3(ah, al, bh, bl, dims):
    return dot(ah, bh, dims) + dot(al, bh, dims) + dot(ah, bl, dims)


def lanes(rows):
    return lax.broadcasted_iota(jnp.int32, (rows, 128), 1)


def pick(tile, get):
    lane = lanes(8)
    value = None
    for p in range(128 * tile // LT, (128 * tile + 127) // LT + 1):
        value = get(p) if value is None else jnp.where(lane < LT * p - 128 * tile, value, get(p))
    return value


def ring(tiles, shift):
    whole, part = divmod(shift % (128 * MAIN), 128)
    if part == 0:
        return [tiles[(t + whole) % MAIN] for t in range(MAIN)]
    lane = lanes(8)
    rolled = [pltpu.roll(x, 128 - part, 1) for x in tiles]
    return [
        jnp.where(lane < 128 - part, rolled[(t + whole) % MAIN], rolled[(t + whole + 1) % MAIN])
        for t in range(MAIN)
    ]


def coordinates():
    w = lax.axis_index("wave")
    v = lax.axis_index("lev")
    return 2 * (v // 4) + w // 8, lax.rem(v, 4), lax.rem(w // 2, 4), lax.rem(w, 2)


def each_peer(visit):
    x, y, z, core = coordinates()
    xs = [lax.rem(x + a, 4) for a in range(4)]
    wave_x = [8 * lax.rem(a, 2) for a in xs]
    lev_x = [4 * (a // 2) for a in xs]
    lev_y = [lax.rem(y + b, 4) for b in range(4)]

    def outer(j, carry):
        wave_c = lax.rem(core + j // 4, 2)
        wave_z = [2 * lax.rem(z + j + d, 4) + wave_c for d in range(4)]
        for i in range(1, 16):
            a, b = i % 4, i // 4
            visit(wave_x[a] + wave_z[(b + 2 * a) % 4], lev_x[a] + lev_y[(a + b) % 4])
        return carry

    lax.fori_loop(0, 8, outer, 0)
    for j in range(1, 8):
        visit(wave_x[0] + 2 * lax.rem(z + j, 4) + lax.rem(core + j // 4, 2), lev_x[0] + lev_y[0])


def kernel(
    waves, waves_row, damp_row, circle, modes_in, modes_out, order, order_t, grid, plm,
    gf, th, tl, rth, rtl,
    gh, gl, pf, ph, pw, s1, r1, s2, r2, x, e, acc, modes, damp,
    circle_v, min_v, mout_v, order_v, order_tv, near_cos, near_sin, far,
    load_sem, send1, recv1, send2, recv2,
):
    w = lax.axis_index("wave")
    v = lax.axis_index("lev")
    me = w * LEVS + v

    small = [
        pltpu.make_async_copy(a, b, load_sem.at[2 + i])
        for i, (a, b) in enumerate(
            [
                (circle, circle_v), (modes_in, min_v), (modes_out, mout_v),
                (order, order_v), (order_t, order_tv),
            ]
        )
    ]
    small[0].start()
    for p in range(16):
        pltpu.make_async_copy(
            grid.at[lax.rem(p - w + 16, 16)], gf.at[pl.ds(LT * p, LT)], load_sem.at[0]
        ).start()
    for s in range(SLOTS):
        pltpu.make_async_copy(
            grid.at[16], gf.at[pl.ds(16 * LT + LT * s, LT)], load_sem.at[0]
        ).start()

    barrier = pltpu.get_barrier_semaphore()

    def greet(to_wave, to_lev):
        pl.semaphore_signal(barrier, inc=1, device_id=(to_wave, to_lev), device_id_type=MESH)

    each_peer(greet)
    for copy in small[1:]:
        copy.start()
    for s in range(SLOTS):
        pltpu.make_async_copy(plm.at[s], pf.at[pl.ds(LAT * s, LAT)], load_sem.at[1]).start()

    slots = DEVS * SLOTS
    eye = lax.broadcasted_iota(jnp.int32, (slots, slots), 0) == lax.broadcasted_iota(
        jnp.int32, (slots, slots), 1
    )
    column = jnp.sum(
        jnp.where(eye, waves_row[...].astype(f32), 0.0), axis=1, keepdims=True
    ).astype(jnp.int32)
    chosen = (lax.broadcasted_iota(jnp.int32, (slots, slots), 1) == column).astype(bf16)
    small[0].wait()
    rest = circle_v[...]
    top, _ = split(rest)
    rest = rest - top.astype(f32)
    mid, low = split(rest)
    rows3 = dot(chosen, top, NN) + dot(chosen, mid, NN) + dot(chosen, low, NN)
    near_cos[...] = rows3[:, 0:128]
    near_sin[...] = rows3[:, 128:256]
    far[...] = rows3[:, 256:384]

    for s in range(SLOTS):

        def table(i, carry):
            mine = pl.ds(s + 96 * i, 32, SLOTS)
            rows = pl.ds(pl.multiple_of(32 * i + 128 * s, 32), 32)
            rows_sin = pl.ds(pl.multiple_of(32 * i + 128 * s + 384, 32), 32)
            c1, n1, f = near_cos[mine, :], near_sin[mine, :], far[mine, :]
            for a in range(LON // 128):
                ca, sa = f[:, a : a + 1], f[:, 16 + a : 17 + a]
                col = slice(128 * a, 128 * a + 128)
                hi, lo = split(c1 * ca - n1 * sa)
                th[rows, col] = hi
                tl[rows, col] = lo
                hi, lo = split(-(n1 * ca + c1 * sa))
                th[rows_sin, col] = hi
                tl[rows_sin, col] = lo
            return carry

        lax.fori_loop(0, 4, table, 0)

    pltpu.make_async_copy(gf.at[pl.ds(0, 760)], gf.at[pl.ds(0, 760)], load_sem.at[0]).wait()
    gf[760:768, :] = jnp.zeros((8, LON), f32)

    def split_grid(i, carry):
        rows = pl.ds(pl.multiple_of(32 * i, 32), 32)
        gh[rows, :], gl[rows, :] = split(gf[rows, :])
        return carry

    lax.fori_loop(0, 24, split_grid, 0)

    lane128 = lanes(128)

    def forward_dft(c):
        def step(n, carry):
            cols = pl.ds(pl.multiple_of(256 * n, 256), 256)
            part = slice(384 * c, 384 * c + 384)
            y = dot3(th[part, :], tl[part, :], gh[cols, :], gl[cols, :], NT)
            for h in range(2):
                yh = y[:, 128 * h : 128 * h + 128]

                def main():
                    for s in range(SLOTS):
                        start = HALF * c + MAIN * s + 2 * n + h
                        s1[pl.ds(start, DEVS, ROWS), :] = yh[128 * s : 128 * s + 128]

                if h == 0:
                    main()
                else:
                    pl.when(n < 2)(main)

                    @pl.when(n == 2)
                    def _():
                        last = jnp.where(
                            lane128 < LT,
                            yh[0:128],
                            jnp.where(lane128 < 2 * LT, yh[128:256], yh[256:384]),
                        )
                        s1[pl.ds(HALF * c + ROWS - 1, DEVS, ROWS), :] = last

            return carry

        lax.fori_loop(0, 3, step, 0)

    def block(c, d):
        return pl.ds(pl.multiple_of((c * DEVS + d) * ROWS, ROWS), ROWS)

    def send(c, src, dst, send_sem, recv_sem):
        pltpu.make_async_copy(src.at[block(c, me)], dst.at[block(c, me)], recv_sem.at[c]).start()

        def go(to_wave, to_lev):
            pltpu.make_async_remote_copy(
                src_ref=src.at[block(c, to_wave * LEVS + to_lev)],
                dst_ref=dst.at[block(c, me)],
                send_sem=send_sem.at[c],
                recv_sem=recv_sem.at[c],
                device_id=(to_wave, to_lev),
                device_id_type=MESH,
            ).start()

        each_peer(go)

    def arrive(c, dst, recv_sem):
        half = dst.at[pl.ds(HALF * c, HALF)]
        pltpu.make_async_copy(half, half, recv_sem.at[c]).wait()

    def sent(c, src, send_sem):
        part = src.at[pl.ds(0, HALF - ROWS)]
        pltpu.make_async_copy(part, part, send_sem.at[c]).wait()

    forward_dft(0)
    pl.semaphore_wait(barrier, DEVS - 1)
    send(0, s1, r1, send1, recv1)
    forward_dft(1)
    send(1, s1, r1, send1, recv1)

    pltpu.make_async_copy(pf, pf, load_sem.at[1]).wait()

    def split_plm(i, carry):
        rows = pl.ds(pl.multiple_of(64 * i, 64), 64)
        ph[rows, :], pw[rows, :] = split(pf[rows, :])
        return carry

    lax.fori_loop(0, SLOTS * LAT // 64, split_plm, 0)

    for copy in small[1:]:
        copy.wait()
    pad = PAD - LEVELS
    for i, part in enumerate(split(jnp.concatenate([min_v[...], jnp.zeros((pad, LEVELS), f32)], 0))):
        modes[i] = dot(part, order_v[...].astype(bf16), NN).astype(bf16)
    for i, part in enumerate(split(jnp.concatenate([mout_v[...], jnp.zeros((LEVELS, pad), f32)], 1))):
        modes[2 + i] = dot(order_tv[...].astype(bf16), part, NN).astype(bf16)
    eye = lax.broadcasted_iota(jnp.int32, (PAD, LEVELS), 0) == lax.broadcasted_iota(
        jnp.int32, (PAD, LEVELS), 1
    )
    damp[...] = jnp.sum(jnp.where(eye, damp_row[...], 0.0), axis=1, keepdims=True)
    x[LEVELS:PAD, :] = jnp.zeros((PAD - LEVELS, LAT), f32)
    lane8 = lanes(8)

    def middle(c):
        acc[...] = jnp.zeros((WAVES * 8, 128), f32)

        def slot(s, carry):
            base = HALF * c + MAIN * s
            for k in range(16):
                tiles = [
                    pick(t, lambda p: r1[pl.ds(base + ((p - k) % 16) * 128 + t, 8, ROWS), :])
                    for t in range(MAIN)
                ]
                for t, value in enumerate(ring(tiles, LT * k)):
                    x[8 * k : 8 * k + 8, 128 * t : 128 * t + 128] = value
            tiles = [None] * MAIN
            for q in range(WAVES):
                own = r1[pl.ds(HALF * c + q * 128 + ROWS - 1, 8, ROWS), :]
                own = pltpu.roll(own, lax.rem(LT * q - LT * s + 768, 128), 1)
                t, off = divmod(LT * q, 128)
                tiles[t] = own if off == 0 else jnp.where(lane8 < off, tiles[t], own)
                if off + LT > 128:
                    tiles[t + 1] = own
            for t in range(MAIN):
                x[128:136, 128 * t : 128 * t + 128] = tiles[t]

            prow = pl.ds(pl.multiple_of(LAT * s, LAT), LAT)
            xh, xl = split(x[...])
            spec = dot3(xh, xl, ph[prow, :], pw[prow, :], NN)
            degree = waves[SLOTS * me + s] + lax.broadcasted_iota(jnp.int32, (PAD, COEFF), 1)
            growth = (degree * (degree + 1)).astype(f32)
            factor = jnp.where(degree < COEFF, 1.0 / (1.0 + damp[...] * growth), 0.0)
            sh, sl = split(spec)
            modal = dot3(modes[0], modes[1], sh, sl, NN) * factor
            mh, ml = split(modal)
            solved = dot3(modes[2], modes[3], mh, ml, NN)
            vh, vl = split(solved)
            x[...] = dot3(vh, vl, ph[prow, :], pw[prow, :], NT)

            for k in range(16):
                tiles = [x[8 * k : 8 * k + 8, 128 * t : 128 * t + 128] for t in range(MAIN)]
                for t, value in enumerate(ring(tiles, -LT * k)):
                    e[8 * k : 8 * k + 8, 128 * t : 128 * t + 128] = value
            for q in range(WAVES):
                for t in range(MAIN):

                    def get(p):
                        k = (p - q) % 16
                        return e[8 * k : 8 * k + 8, 128 * t : 128 * t + 128]

                    s2[pl.ds(base + q * 128 + t, 8, ROWS), :] = pick(t, get)
                t, off = divmod(LT * q, 128)
                own = x[128:136, 128 * t : 128 * t + 128]
                if off + LT > 128:
                    after = x[128:136, 128 * t + 128 : 128 * t + 256]
                    own = jnp.where(lane8 < off, after, own)
                own = pltpu.roll(own, lax.rem(LT * s - LT * q + 768, 128), 1)
                inside = (lane8 >= LT * s) & (lane8 < LT * s + LT)
                acc[8 * q : 8 * q + 8, :] = jnp.where(inside, own, acc[8 * q : 8 * q + 8, :])
            return carry

        lax.fori_loop(0, SLOTS, slot, 0)
        s2[pl.ds(HALF * c + ROWS - 1, DEVS, ROWS), :] = acc[...]

    for c in range(2):
        arrive(c, r1, recv1)
        middle(c)
        send(c, s2, r2, send2, recv2)

    def transpose(c):
        for s in range(SLOTS):
            for t in range(MAIN):
                tile = r2[pl.ds(HALF * c + MAIN * s + t, DEVS, ROWS), :]
                hi, lo = split(tile.T)
                rth[128 * t : 128 * t + 128, 128 * s : 128 * s + 128] = hi
                rtl[128 * t : 128 * t + 128, 128 * s : 128 * s + 128] = lo
            tile = r2[pl.ds(HALF * c + ROWS - 1, DEVS, ROWS), :]
            inside = (lane128 >= LT * s) & (lane128 < LT * s + LT)
            hi, lo = split(jnp.where(inside, tile, 0.0).T)
            rth[128 * MAIN :, 128 * s : 128 * s + 128] = hi
            rtl[128 * MAIN :, 128 * s : 128 * s + 128] = lo

    arrive(0, r2, recv2)
    transpose(0)

    def adjoint(n, carry):
        cols = pl.ds(pl.multiple_of(256 * n, 256), 256)
        gf[:, cols] = dot3(rth[...], rtl[...], th[0:384, cols], tl[0:384, cols], NN)
        return carry

    lax.fori_loop(0, LON // 256, adjoint, 0)
    for c in range(2):
        sent(c, s1, send1)
        sent(c, s2, send2)
    arrive(1, r2, recv2)
    transpose(1)


def finish(gf, th, tl, rth, rtl, out, block, sem):
    w = lax.axis_index("wave")
    copies = []
    for n in range(LON // 256):
        cols = slice(256 * n, 256 * n + 256)
        y = gf[:, cols] + dot3(rth[...], rtl[...], th[384:768, cols], tl[384:768, cols], NN)
        for p in range(16):
            level = lax.rem(p - w + 16, 16)
            block[n, pl.ds(pl.multiple_of(LT * level, 8), LT), :] = y[LT * p : LT * p + LT]
        block[n, 640:680, :] = y[640:680] + y[680:720] + y[720:760]
        copy = pltpu.make_async_copy(block.at[n], out.at[:, cols], sem.at[n])
        copy.start()
        copies.append(copy)
    for copy in copies:
        copy.wait()


def circle_table():
    wave = np.arange(DEVS * SLOTS)[:, None]
    near = 2.0 * math.pi / LON * (wave * np.arange(128)[None, :] % LON)
    far = 2.0 * math.pi / 10 * (wave * np.arange(16)[None, :] % 10)
    table = np.zeros((DEVS * SLOTS, 384))
    table[:, :128] = np.cos(near) / math.sqrt(LON)
    table[:, 128:256] = np.sin(near) / math.sqrt(LON)
    table[:, 256:272] = np.cos(far)
    table[:, 272:288] = np.sin(far)
    return table.astype(np.float32)


def level_order():
    matrix = np.zeros((LEVELS, PAD), np.float32)
    level = np.arange(LEVELS)
    matrix[level, level % LV * LEVS + level // LV] = 1
    return matrix


def local(grid_in, wavenumbers, legendre, modes_in, modes_out, damping):
    order = level_order()
    vmem = pl.BlockSpec(memory_space=pltpu.VMEM)
    hbm = pl.BlockSpec(memory_space=pl.ANY)
    dma = pltpu.SemaphoreType.DMA
    held = pl.pallas_call(
        kernel,
        out_shape=[
            pltpu.VMEM((768, LON), f32),
            pltpu.VMEM((768, LON), bf16),
            pltpu.VMEM((768, LON), bf16),
            pltpu.VMEM((768, 384), bf16),
            pltpu.VMEM((768, 384), bf16),
        ],
        in_specs=[pl.BlockSpec(memory_space=pltpu.SMEM)] + [vmem] * 2 + [hbm] * 7,
        out_specs=[vmem] * 5,
        scratch_shapes=[
            pltpu.VMEM((768, LON), bf16),
            pltpu.VMEM((768, LON), bf16),
            pltpu.VMEM((SLOTS * LAT, COEFF), f32),
            pltpu.VMEM((SLOTS * LAT, COEFF), bf16),
            pltpu.VMEM((SLOTS * LAT, COEFF), bf16),
            pltpu.VMEM((2 * HALF, 128), f32),
            pltpu.VMEM((2 * HALF, 128), f32),
            pltpu.VMEM((2 * HALF, 128), f32),
            pltpu.VMEM((2 * HALF, 128), f32),
            pltpu.VMEM((PAD, LAT), f32),
            pltpu.VMEM((128, LAT), f32),
            pltpu.VMEM((WAVES * 8, 128), f32),
            pltpu.VMEM((4, PAD, PAD), bf16),
            pltpu.VMEM((PAD, 1), f32),
            pltpu.VMEM((DEVS * SLOTS, 384), f32),
            pltpu.VMEM((LEVELS, LEVELS), f32),
            pltpu.VMEM((LEVELS, LEVELS), f32),
            pltpu.VMEM((LEVELS, PAD), f32),
            pltpu.VMEM((PAD, LEVELS), f32),
            pltpu.VMEM((DEVS * SLOTS, 128), f32),
            pltpu.VMEM((DEVS * SLOTS, 128), f32),
            pltpu.VMEM((DEVS * SLOTS, 128), f32),
            dma((7,)),
            dma((2,)),
            dma((2,)),
            dma((2,)),
            dma((2,)),
        ],
        compiler_params=pltpu.CompilerParams(
            collective_id=0, has_side_effects=True, vmem_limit_bytes=48 << 20
        ),
        name="spectral_step",
    )(
        wavenumbers, wavenumbers.reshape(1, -1), damping.reshape(1, -1), jnp.asarray(circle_table()),
        modes_in, modes_out, jnp.asarray(order), jnp.asarray(order.T.copy()),
        grid_in.reshape(LV, LT, LON), legendre,
    )
    result = pl.pallas_call(
        finish,
        out_shape=jax.ShapeDtypeStruct((LV * LT, LON), f32),
        in_specs=[vmem] * 5,
        out_specs=hbm,
        scratch_shapes=[
            pltpu.VMEM((LON // 256, LV * LT, 256), f32),
            dma((LON // 256,)),
        ],
        compiler_params=pltpu.CompilerParams(vmem_limit_bytes=40 << 20),
        name="finish",
    )(*[pltpu.with_memory_space_constraint(a, pltpu.VMEM) for a in held])
    return result.reshape(1, LV, LT, LON)


def solution(mesh):
    return jax.shard_map(
        local,
        mesh=mesh,
        in_specs=(P(None, "lev", "wave", None), P(), P(("wave", "lev"), None, None), P(), P(), P()),
        out_specs=P(None, "lev", "wave", None),
        check_vma=False,
    )
```

```python
import math

import jax
import jax.numpy as jnp
import numpy as np
from jax import lax
from jax.experimental import pallas as pl
from jax.experimental.pallas import tpu as pltpu
from jax.sharding import PartitionSpec as P

MESH = pl.DeviceIdType.MESH
f32 = jnp.float32
bf16 = jnp.bfloat16

LON = 1280
LAT = 640
COEFF = 640
WAVES = 16
LEVS = 8
DEVS = WAVES * LEVS
LV = 17
LT = 40
SLOTS = 3
LEVELS = LEVS * LV
PAD = 144
ROWS = 16
HALF = DEVS * ROWS
MAIN = 16 * LT // 128


def split(x):
    hi = x.astype(bf16)
    return hi, (x - hi.astype(f32)).astype(bf16)


def dot(a, b, dims):
    return lax.dot_general(a, b, (dims, ((), ())), preferred_element_type=f32)


TN = ((0,), (0,))
NN = ((1,), (0,))
NT = ((1,), (1,))


def dot3(ah, al, bh, bl, dims):
    return dot(ah, bh, dims) + dot(al, bh, dims) + dot(ah, bl, dims)


def lanes(rows):
    return lax.broadcasted_iota(jnp.int32, (rows, 128), 1)


def pick(tile, get):
    lane = lanes(8)
    value = None
    for p in range(128 * tile // LT, (128 * tile + 127) // LT + 1):
        value = get(p) if value is None else jnp.where(lane < LT * p - 128 * tile, value, get(p))
    return value


def ring(tiles, shift):
    whole, part = divmod(shift % (128 * MAIN), 128)
    if part == 0:
        return [tiles[(t + whole) % MAIN] for t in range(MAIN)]
    lane = lanes(8)
    rolled = [pltpu.roll(x, 128 - part, 1) for x in tiles]
    return [
        jnp.where(lane < 128 - part, rolled[(t + whole) % MAIN], rolled[(t + whole + 1) % MAIN])
        for t in range(MAIN)
    ]


def coordinates():
    w = lax.axis_index("wave")
    v = lax.axis_index("lev")
    return 2 * (v // 4) + w // 8, lax.rem(v, 4), lax.rem(w // 2, 4), lax.rem(w, 2)


def each_peer(visit):
    x, y, z, core = coordinates()
    xs = [lax.rem(x + a, 4) for a in range(4)]
    wave_x = [8 * lax.rem(a, 2) for a in xs]
    lev_x = [4 * (a // 2) for a in xs]
    lev_y = [lax.rem(y + b, 4) for b in range(4)]

    def outer(j, carry):
        wave_c = lax.rem(core + j // 4, 2)
        wave_z = [2 * lax.rem(z + j + d, 4) + wave_c for d in range(4)]
        for i in range(1, 16):
            a, b = i % 4, i // 4
            visit(wave_x[a] + wave_z[(b + 2 * a) % 4], lev_x[a] + lev_y[(a + b) % 4])
        return carry

    lax.fori_loop(0, 8, outer, 0)
    for j in range(1, 8):
        visit(wave_x[0] + 2 * lax.rem(z + j, 4) + lax.rem(core + j // 4, 2), lev_x[0] + lev_y[0])


def kernel(
    waves, waves_all, damp_row, circle, modes_in, modes_out, order, order_t, grid, plm,
    gf, th, tl, rth, rtl,
    gh, gl, pf, ph, pw, s1, r1, s2, r2, x, e, acc, modes, damp,
    circle_v, min_v, mout_v, order_v, order_tv, near_cos, near_sin, far, waves_row,
    load_sem, send1, recv1, send2, recv2,
):
    w = lax.axis_index("wave")
    v = lax.axis_index("lev")
    me = w * LEVS + v

    small = [
        pltpu.make_async_copy(a, b, load_sem.at[2 + i])
        for i, (a, b) in enumerate(
            [
                (circle, circle_v), (modes_in, min_v), (modes_out, mout_v),
                (order, order_v), (order_t, order_tv),
            ]
        )
    ]
    row_copy = pltpu.make_async_copy(waves_all, waves_row.at[0], load_sem.at[7])
    row_copy.start()
    small[0].start()
    for p in range(16):
        pltpu.make_async_copy(
            grid.at[lax.rem(p - w + 16, 16)], gf.at[pl.ds(128 + LT * p, LT)], load_sem.at[0]
        ).start()
    for s in range(SLOTS):
        pltpu.make_async_copy(
            grid.at[16], gf.at[pl.ds(LT * s, LT)], load_sem.at[0]
        ).start()

    barrier = pltpu.get_barrier_semaphore()

    def greet(to_wave, to_lev):
        pl.semaphore_signal(barrier, inc=1, device_id=(to_wave, to_lev), device_id_type=MESH)

    each_peer(greet)
    for copy in small[1:]:
        copy.start()
    for s in range(SLOTS):
        pltpu.make_async_copy(plm.at[s], pf.at[pl.ds(LAT * s, LAT)], load_sem.at[1]).start()

    slots = DEVS * SLOTS
    eye = lax.broadcasted_iota(jnp.int32, (slots, slots), 0) == lax.broadcasted_iota(
        jnp.int32, (slots, slots), 1
    )
    row_copy.wait()
    column = jnp.sum(
        jnp.where(eye, waves_row[...].astype(f32), 0.0), axis=1, keepdims=True
    ).astype(jnp.int32)
    chosen = (lax.broadcasted_iota(jnp.int32, (slots, slots), 1) == column).astype(bf16)
    small[0].wait()
    rest = circle_v[...]
    top, _ = split(rest)
    rest = rest - top.astype(f32)
    mid, low = split(rest)
    rows3 = dot(chosen, top, NN) + dot(chosen, mid, NN) + dot(chosen, low, NN)
    near_cos[...] = rows3[:, 0:128]
    near_sin[...] = rows3[:, 128:256]
    far[...] = rows3[:, 256:384]

    def make_table(c):
        for s in range(SLOTS):

            def table(i, carry):
                mine = pl.ds(s + 96 * i, 32, SLOTS)
                rows = pl.ds(pl.multiple_of(32 * i + 128 * s + 384 * c, 32), 32)
                c1, n1, f = near_cos[mine, :], near_sin[mine, :], far[mine, :]
                for a in range(LON // 128):
                    ca, sa = f[:, a : a + 1], f[:, 16 + a : 17 + a]
                    value = c1 * ca - n1 * sa if c == 0 else -(n1 * ca + c1 * sa)
                    col = slice(128 * a, 128 * a + 128)
                    th[rows, col], tl[rows, col] = split(value)
                return carry

            lax.fori_loop(0, 4, table, 0)

    make_table(0)

    pltpu.make_async_copy(gf.at[pl.ds(0, 760)], gf.at[pl.ds(0, 760)], load_sem.at[0]).wait()
    gf[120:128, :] = jnp.zeros((8, LON), f32)

    def split_grid(i, carry):
        rows = pl.ds(pl.multiple_of(32 * i, 32), 32)
        gh[rows, :], gl[rows, :] = split(gf[rows, :])
        return carry

    lax.fori_loop(0, 24, split_grid, 0)

    lane128 = lanes(128)

    def forward_dft(c, n):
        cols = slice(256 * n, 256 * n + 256)
        part = slice(384 * c, 384 * c + 384)
        y = dot3(th[part, :], tl[part, :], gh[cols, :], gl[cols, :], NT)
        for h in range(2):
            yh = y[:, 128 * h : 128 * h + 128]
            t = 2 * n + h - 1
            if t >= 0:
                for s in range(SLOTS):
                    start = HALF * c + 1 + 3 * t + s
                    s1[pl.ds(start, DEVS, ROWS), :] = yh[128 * s : 128 * s + 128]
            else:
                last = jnp.where(
                    lane128 < LT,
                    yh[0:128],
                    jnp.where(lane128 < 2 * LT, yh[128:256], yh[256:384]),
                )
                s1[pl.ds(HALF * c, DEVS, ROWS), :] = last

    def send(c, first, rows, index, src, dst, send_sem, recv_sem):
        def block(d):
            return pl.ds(pl.multiple_of((c * DEVS + d) * ROWS + first, rows), rows)

        pltpu.make_async_copy(src.at[block(me)], dst.at[block(me)], recv_sem.at[index]).start()

        def go(to_wave, to_lev):
            pltpu.make_async_remote_copy(
                src_ref=src.at[block(to_wave * LEVS + to_lev)],
                dst_ref=dst.at[block(me)],
                send_sem=send_sem.at[index],
                recv_sem=recv_sem.at[index],
                device_id=(to_wave, to_lev),
                device_id_type=MESH,
            ).start()

        each_peer(go)

    def arrive(rows, index, dst, recv_sem):
        part = dst.at[pl.ds(0, DEVS * rows)]
        pltpu.make_async_copy(part, part, recv_sem.at[index]).wait()

    def sent(rows, index, src, send_sem):
        part = src.at[pl.ds(0, (DEVS - 1) * rows)]
        pltpu.make_async_copy(part, part, send_sem.at[index]).wait()

    forward_dft(0, 0)
    forward_dft(0, 1)
    pl.semaphore_wait(barrier, DEVS - 1)
    send(0, 0, 8, 0, s1, r1, send1, recv1)
    forward_dft(0, 2)
    send(0, 8, 8, 1, s1, r1, send1, recv1)
    make_table(1)
    for n in range(3):
        forward_dft(1, n)
    send(1, 0, 16, 2, s1, r1, send1, recv1)

    pltpu.make_async_copy(pf, pf, load_sem.at[1]).wait()

    def split_plm(i, carry):
        rows = pl.ds(pl.multiple_of(64 * i, 64), 64)
        ph[rows, :], pw[rows, :] = split(pf[rows, :])
        return carry

    lax.fori_loop(0, SLOTS * LAT // 64, split_plm, 0)

    for copy in small[1:]:
        copy.wait()
    pad = PAD - LEVELS
    for i, part in enumerate(split(jnp.concatenate([min_v[...], jnp.zeros((pad, LEVELS), f32)], 0))):
        modes[i] = dot(part, order_v[...].astype(bf16), NN).astype(bf16)
    for i, part in enumerate(split(jnp.concatenate([mout_v[...], jnp.zeros((LEVELS, pad), f32)], 1))):
        modes[2 + i] = dot(order_tv[...].astype(bf16), part, NN).astype(bf16)
    eye = lax.broadcasted_iota(jnp.int32, (PAD, LEVELS), 0) == lax.broadcasted_iota(
        jnp.int32, (PAD, LEVELS), 1
    )
    damp[...] = jnp.sum(jnp.where(eye, damp_row[...], 0.0), axis=1, keepdims=True)
    x[LEVELS:PAD, :] = jnp.zeros((PAD - LEVELS, LAT), f32)
    lane8 = lanes(8)

    def middle(c):
        acc[...] = jnp.zeros((WAVES * 8, 128), f32)

        def slot(s, carry):
            base = HALF * c + 1 + s
            for k in range(16):
                tiles = [
                    pick(t, lambda p: r1[pl.ds(base + ((p - k) % 16) * 128 + 3 * t, 8, ROWS), :])
                    for t in range(MAIN)
                ]
                for t, value in enumerate(ring(tiles, LT * k)):
                    x[8 * k : 8 * k + 8, 128 * t : 128 * t + 128] = value
            tiles = [None] * MAIN
            for q in range(WAVES):
                own = r1[pl.ds(HALF * c + q * 128, 8, ROWS), :]
                own = pltpu.roll(own, lax.rem(LT * q - LT * s + 768, 128), 1)
                t, off = divmod(LT * q, 128)
                tiles[t] = own if off == 0 else jnp.where(lane8 < off, tiles[t], own)
                if off + LT > 128:
                    tiles[t + 1] = own
            for t in range(MAIN):
                x[128:136, 128 * t : 128 * t + 128] = tiles[t]

            prow = pl.ds(pl.multiple_of(LAT * s, LAT), LAT)
            xh, xl = split(x[...])
            spec = dot3(xh, xl, ph[prow, :], pw[prow, :], NN)
            degree = waves[SLOTS * me + s] + lax.broadcasted_iota(jnp.int32, (PAD, COEFF), 1)
            growth = (degree * (degree + 1)).astype(f32)
            factor = jnp.where(degree < COEFF, 1.0 / (1.0 + damp[...] * growth), 0.0)
            sh, sl = split(spec)
            modal = dot3(modes[0], modes[1], sh, sl, NN) * factor
            mh, ml = split(modal)
            solved = dot3(modes[2], modes[3], mh, ml, NN)
            vh, vl = split(solved)
            x[...] = dot3(vh, vl, ph[prow, :], pw[prow, :], NT)

            for k in range(16):
                tiles = [x[8 * k : 8 * k + 8, 128 * t : 128 * t + 128] for t in range(MAIN)]
                for t, value in enumerate(ring(tiles, -LT * k)):
                    e[8 * k : 8 * k + 8, 128 * t : 128 * t + 128] = value
            for q in range(WAVES):
                for t in range(MAIN):

                    def get(p):
                        k = (p - q) % 16
                        return e[8 * k : 8 * k + 8, 128 * t : 128 * t + 128]

                    s2[pl.ds(base + q * 128 + 3 * t, 8, ROWS), :] = pick(t, get)
                t, off = divmod(LT * q, 128)
                own = x[128:136, 128 * t : 128 * t + 128]
                if off + LT > 128:
                    after = x[128:136, 128 * t + 128 : 128 * t + 256]
                    own = jnp.where(lane8 < off, after, own)
                own = pltpu.roll(own, lax.rem(LT * s - LT * q + 768, 128), 1)
                inside = (lane8 >= LT * s) & (lane8 < LT * s + LT)
                acc[8 * q : 8 * q + 8, :] = jnp.where(inside, own, acc[8 * q : 8 * q + 8, :])
            return carry

        lax.fori_loop(0, SLOTS, slot, 0)
        s2[pl.ds(HALF * c, DEVS, ROWS), :] = acc[...]

    arrive(8, 0, r1, recv1)
    arrive(8, 1, r1, recv1)
    middle(0)
    send(0, 0, 16, 2, s2, r2, send2, recv2)
    arrive(16, 2, r1, recv1)
    middle(1)
    send(1, 0, 8, 0, s2, r2, send2, recv2)
    send(1, 8, 8, 1, s2, r2, send2, recv2)

    def transpose(c, tiles):
        for t in tiles:
            for s in range(SLOTS):
                if t < 0:
                    tile = r2[pl.ds(HALF * c, DEVS, ROWS), :]
                    tile = jnp.where((lane128 >= LT * s) & (lane128 < LT * s + LT), tile, 0.0)
                else:
                    tile = r2[pl.ds(HALF * c + 1 + 3 * t + s, DEVS, ROWS), :]
                where = (slice(128 * t + 128, 128 * t + 256), slice(128 * s, 128 * s + 128))
                rth[where], rtl[where] = split(tile.T)

    arrive(16, 2, r2, recv2)
    transpose(0, range(-1, MAIN))

    def adjoint(n, carry):
        cols = pl.ds(pl.multiple_of(256 * n, 256), 256)
        gf[:, cols] = dot3(rth[...], rtl[...], th[0:384, cols], tl[0:384, cols], NN)
        return carry

    lax.fori_loop(0, LON // 256, adjoint, 0)
    for index, rows in ((0, 8), (1, 8), (2, 16)):
        sent(rows, index, s1, send1)
    sent(16, 2, s2, send2)
    arrive(8, 0, r2, recv2)
    transpose(1, range(-1, 2))

    def adjoint_rest(n, carry):
        cols = pl.ds(pl.multiple_of(256 * n, 256), 256)
        gf[0:384, cols] += dot3(
            rth[0:384, :], rtl[0:384, :], th[384:768, cols], tl[384:768, cols], NN
        )
        return carry

    lax.fori_loop(0, LON // 256, adjoint_rest, 0)
    gf[0:40, :] = gf[0:40, :] + gf[40:80, :] + gf[80:120, :]
    sent(8, 0, s2, send2)
    arrive(8, 1, r2, recv2)
    transpose(1, range(2, MAIN))
    sent(8, 1, s2, send2)


def finish(gf, th, tl, rth, rtl, out, rest, sem):
    w = lax.axis_index("wave")
    copies = []

    def write(src, dst, index):
        copy = pltpu.make_async_copy(src, dst, sem.at[index])
        copy.start()
        copies.append(copy)

    write(gf.at[pl.ds(0, LT)], out.at[16], 0)
    for p in range(6):
        write(gf.at[pl.ds(128 + LT * p, LT)], out.at[lax.rem(p - w + 16, 16)], 1 + p)
    rest[0:16, :] = gf[368:384, :]
    index = 7
    for cols in (slice(0, 512), slice(512, 1024), slice(1024, 1280)):
        rest[16:400, cols] = gf[384:768, cols] + dot3(
            rth[384:768, :], rtl[384:768, :], th[384:768, cols], tl[384:768, cols], NN
        )
        for p in range(6, 16):
            write(
                rest.at[pl.ds(LT * (p - 6), LT), cols],
                out.at[lax.rem(p - w + 16, 16), :, cols],
                index,
            )
            index += 1
    for copy in copies:
        copy.wait()


def circle_table():
    wave = np.arange(DEVS * SLOTS)[:, None]
    near = 2.0 * math.pi / LON * (wave * np.arange(128)[None, :] % LON)
    far = 2.0 * math.pi / 10 * (wave * np.arange(16)[None, :] % 10)
    table = np.zeros((DEVS * SLOTS, 384))
    table[:, :128] = np.cos(near) / math.sqrt(LON)
    table[:, 128:256] = np.sin(near) / math.sqrt(LON)
    table[:, 256:272] = np.cos(far)
    table[:, 272:288] = np.sin(far)
    return table.astype(np.float32)


def level_order():
    matrix = np.zeros((LEVELS, PAD), np.float32)
    level = np.arange(LEVELS)
    matrix[level, level % LV * LEVS + level // LV] = 1
    return matrix


def local(grid_in, wavenumbers, legendre, modes_in, modes_out, damping):
    order = level_order()
    vmem = pl.BlockSpec(memory_space=pltpu.VMEM)
    hbm = pl.BlockSpec(memory_space=pl.ANY)
    dma = pltpu.SemaphoreType.DMA
    held = pl.pallas_call(
        kernel,
        out_shape=[
            pltpu.VMEM((768, LON), f32),
            pltpu.VMEM((768, LON), bf16),
            pltpu.VMEM((768, LON), bf16),
            pltpu.VMEM((768, 384), bf16),
            pltpu.VMEM((768, 384), bf16),
        ],
        in_specs=[pl.BlockSpec(memory_space=pltpu.SMEM), hbm, vmem] + [hbm] * 7,
        out_specs=[vmem] * 5,
        scratch_shapes=[
            pltpu.VMEM((768, LON), bf16),
            pltpu.VMEM((768, LON), bf16),
            pltpu.VMEM((SLOTS * LAT, COEFF), f32),
            pltpu.VMEM((SLOTS * LAT, COEFF), bf16),
            pltpu.VMEM((SLOTS * LAT, COEFF), bf16),
            pltpu.VMEM((2 * HALF, 128), f32),
            pltpu.VMEM((2 * HALF, 128), f32),
            pltpu.VMEM((2 * HALF, 128), f32),
            pltpu.VMEM((2 * HALF, 128), f32),
            pltpu.VMEM((PAD, LAT), f32),
            pltpu.VMEM((128, LAT), f32),
            pltpu.VMEM((WAVES * 8, 128), f32),
            pltpu.VMEM((4, PAD, PAD), bf16),
            pltpu.VMEM((PAD, 1), f32),
            pltpu.VMEM((DEVS * SLOTS, 384), f32),
            pltpu.VMEM((LEVELS, LEVELS), f32),
            pltpu.VMEM((LEVELS, LEVELS), f32),
            pltpu.VMEM((LEVELS, PAD), f32),
            pltpu.VMEM((PAD, LEVELS), f32),
            pltpu.VMEM((DEVS * SLOTS, 128), f32),
            pltpu.VMEM((DEVS * SLOTS, 128), f32),
            pltpu.VMEM((DEVS * SLOTS, 128), f32),
            pltpu.VMEM((1, DEVS * SLOTS), jnp.int32),
            dma((8,)),
            dma((3,)),
            dma((3,)),
            dma((3,)),
            dma((3,)),
        ],
        compiler_params=pltpu.CompilerParams(
            collective_id=0, has_side_effects=True, vmem_limit_bytes=48 << 20
        ),
        name="spectral_step",
    )(
        wavenumbers, wavenumbers, damping.reshape(1, -1), jnp.asarray(circle_table()),
        modes_in, modes_out, jnp.asarray(order), jnp.asarray(order.T.copy()),
        grid_in.reshape(LV, LT, LON), legendre,
    )
    result = pl.pallas_call(
        finish,
        out_shape=jax.ShapeDtypeStruct((LV, LT, LON), f32),
        in_specs=[vmem] * 5,
        out_specs=hbm,
        scratch_shapes=[
            pltpu.VMEM((400, LON), f32),
            dma((37,)),
        ],
        compiler_params=pltpu.CompilerParams(vmem_limit_bytes=40 << 20),
        name="finish",
    )(*[pltpu.with_memory_space_constraint(a, pltpu.VMEM) for a in held])
    return result.reshape(1, LV, LT, LON)


def solution(mesh):
    return jax.shard_map(
        local,
        mesh=mesh,
        in_specs=(P(None, "lev", "wave", None), P(), P(("wave", "lev"), None, None), P(), P(), P()),
        out_specs=P(None, "lev", "wave", None),
        check_vma=False,
    )
```

```python
import math

import jax
import jax.numpy as jnp
import numpy as np
from jax import lax
from jax.experimental import pallas as pl
from jax.experimental.pallas import tpu as pltpu
from jax.sharding import PartitionSpec as P

MESH = pl.DeviceIdType.MESH
f32 = jnp.float32
bf16 = jnp.bfloat16

LON = 1280
LAT = 640
COEFF = 640
WAVES = 16
LEVS = 8
DEVS = WAVES * LEVS
LV = 17
LT = 40
SLOTS = 3
LEVELS = LEVS * LV
PAD = 144
ROWS = 16
HALF = DEVS * ROWS
MAIN = 16 * LT // 128


def split(x):
    hi = x.astype(bf16)
    return hi, (x - hi.astype(f32)).astype(bf16)


def dot(a, b, dims):
    return lax.dot_general(a, b, (dims, ((), ())), preferred_element_type=f32)


TN = ((0,), (0,))
NN = ((1,), (0,))
NT = ((1,), (1,))


def dot3(ah, al, bh, bl, dims):
    rows = ah.shape[0]
    both = dot(jnp.concatenate([ah, al], 0), bh, dims)
    return both[:rows] + both[rows:] + dot(ah, bl, dims)


def dot3_deep(ah, al, bh, bl):
    return dot(jnp.concatenate([ah, al, ah], 1), jnp.concatenate([bh, bh, bl], 0), NN)


def lanes(rows):
    return lax.broadcasted_iota(jnp.int32, (rows, 128), 1)


def pick(tile, get):
    lane = lanes(8)
    value = None
    for p in range(128 * tile // LT, (128 * tile + 127) // LT + 1):
        value = get(p) if value is None else jnp.where(lane < LT * p - 128 * tile, value, get(p))
    return value


def ring(tiles, shift):
    whole, part = divmod(shift % (128 * MAIN), 128)
    if part == 0:
        return [tiles[(t + whole) % MAIN] for t in range(MAIN)]
    lane = lanes(8)
    rolled = [pltpu.roll(x, 128 - part, 1) for x in tiles]
    return [
        jnp.where(lane < 128 - part, rolled[(t + whole) % MAIN], rolled[(t + whole + 1) % MAIN])
        for t in range(MAIN)
    ]


def coordinates():
    w = lax.axis_index("wave")
    v = lax.axis_index("lev")
    return 2 * (v // 4) + w // 8, lax.rem(v, 4), lax.rem(w // 2, 4), lax.rem(w, 2)


def each_peer(visit):
    x, y, z, core = coordinates()
    xs = [lax.rem(x + a, 4) for a in range(4)]
    wave_x = [8 * lax.rem(a, 2) for a in xs]
    lev_x = [4 * (a // 2) for a in xs]
    lev_y = [lax.rem(y + b, 4) for b in range(4)]

    def outer(j, carry):
        wave_c = lax.rem(core + j // 4, 2)
        wave_z = [2 * lax.rem(z + j + d, 4) + wave_c for d in range(4)]
        for i in range(1, 16):
            a, b = i % 4, i // 4
            visit(wave_x[a] + wave_z[(b + 2 * a) % 4], lev_x[a] + lev_y[(a + b) % 4])
        return carry

    lax.fori_loop(0, 8, outer, 0)
    for j in range(1, 8):
        visit(wave_x[0] + 2 * lax.rem(z + j, 4) + lax.rem(core + j // 4, 2), lev_x[0] + lev_y[0])


def kernel(
    waves, waves_all, damp_row, circle, modes_in, modes_out, order, order_t, grid, plm,
    gf, th, tl, rth, rtl,
    gh, gl, pf, ph, pw, s1, r1, s2, r2, x, e, acc, modes, damp,
    circle_v, min_v, mout_v, order_v, order_tv, near_cos, near_sin, far, waves_row,
    load_sem, send1, recv1, send2, recv2,
):
    w = lax.axis_index("wave")
    v = lax.axis_index("lev")
    me = w * LEVS + v

    small = [
        pltpu.make_async_copy(a, b, load_sem.at[2 + i])
        for i, (a, b) in enumerate(
            [
                (circle, circle_v), (modes_in, min_v), (modes_out, mout_v),
                (order, order_v), (order_t, order_tv),
            ]
        )
    ]
    row_copy = pltpu.make_async_copy(waves_all, waves_row.at[0], load_sem.at[7])
    row_copy.start()
    small[0].start()
    for s in range(SLOTS):
        pltpu.make_async_copy(
            grid.at[16], gf.at[pl.ds(LT * s, LT)], load_sem.at[0]
        ).start()

    def load_level(p):
        pltpu.make_async_copy(
            grid.at[lax.rem(p - w + 16, 16)],
            gf.at[pl.ds(128 + LT * p, LT)],
            load_sem.at[0 if p < 4 else 7 + (p + 2) // 6],
        ).start()

    for p in range(4):
        load_level(p)

    barrier = pltpu.get_barrier_semaphore()

    def greet(to_wave, to_lev):
        pl.semaphore_signal(barrier, inc=1, device_id=(to_wave, to_lev), device_id_type=MESH)

    each_peer(greet)
    for p in range(4, 16):
        load_level(p)

    slots = DEVS * SLOTS
    eye = lax.broadcasted_iota(jnp.int32, (slots, slots), 0) == lax.broadcasted_iota(
        jnp.int32, (slots, slots), 1
    )
    row_copy.wait()
    column = jnp.sum(
        jnp.where(eye, waves_row[...].astype(f32), 0.0), axis=1, keepdims=True
    ).astype(jnp.int32)
    chosen = (lax.broadcasted_iota(jnp.int32, (slots, slots), 1) == column).astype(bf16)
    small[0].wait()
    top, rest = split(circle_v[...])
    rows3 = dot(chosen, top, NN) + dot(chosen, rest, NN)
    near_cos[...] = rows3[:, 0:128]
    near_sin[...] = rows3[:, 128:256]
    far[...] = rows3[:, 256:384]

    def make_table(c):
        def table(s, carry):
            mine = pl.ds(s, DEVS, SLOTS)
            rows = pl.ds(pl.multiple_of(384 * c + DEVS * s, DEVS), DEVS)
            cosine, sine, f = near_cos[mine, :], near_sin[mine, :], far[mine, :]
            first = jnp.where(c == 0, cosine, -sine)
            second = jnp.where(c == 0, sine, cosine)
            for a in range(LON // 128):
                ca, sa = f[:, a : a + 1], f[:, 16 + a : 17 + a]
                col = slice(128 * a, 128 * a + 128)
                th[rows, col], tl[rows, col] = split(first * ca - second * sa)
            return carry

        lax.fori_loop(0, SLOTS, table, 0)

    def loaded(rows, index):
        part = gf.at[pl.ds(0, rows)]
        pltpu.make_async_copy(part, part, load_sem.at[index]).wait()

    def split_grid(i, carry):
        rows = pl.ds(pl.multiple_of(32 * i, 32), 32)
        gh[rows, :], gl[rows, :] = split(gf[rows, :])
        return carry

    lane128 = lanes(128)

    def forward_dft(c, n):
        cols = pl.ds(pl.multiple_of(256 * n, 256), 256)
        part = pl.ds(pl.multiple_of(384 * c, 128), 384)
        y = dot3(th[part, :], tl[part, :], gh[cols, :], gl[cols, :], NT)
        y0, y1 = y[:, 0:128], y[:, 128:256]

        @pl.when(n == 0)
        def _():
            last = jnp.where(
                lane128 < LT, y0[0:128], jnp.where(lane128 < 2 * LT, y0[128:256], y0[256:384])
            )
            s1[pl.ds(HALF * c, DEVS, ROWS), :] = last

        @pl.when(n > 0)
        def _():
            for s in range(SLOTS):
                s1[pl.ds(HALF * c + 6 * n - 2 + s, DEVS, ROWS), :] = y0[128 * s : 128 * s + 128]

        for s in range(SLOTS):
            s1[pl.ds(HALF * c + 6 * n + 1 + s, DEVS, ROWS), :] = y1[128 * s : 128 * s + 128]

    def send(c, h, src, dst, send_sem, recv_sem):
        index = 2 * c + h

        def block(d):
            return pl.ds(pl.multiple_of((c * DEVS + d) * ROWS + 8 * h, 8), 8)

        pltpu.make_async_copy(src.at[block(me)], dst.at[block(me)], recv_sem.at[index]).start()

        def go(to_wave, to_lev):
            pltpu.make_async_remote_copy(
                src_ref=src.at[block(to_wave * LEVS + to_lev)],
                dst_ref=dst.at[block(me)],
                send_sem=send_sem.at[index],
                recv_sem=recv_sem.at[index],
                device_id=(to_wave, to_lev),
                device_id_type=MESH,
            ).start()

        each_peer(go)

    def arrive(index, dst, recv_sem):
        part = dst.at[pl.ds(0, DEVS * 8)]
        pltpu.make_async_copy(part, part, recv_sem.at[index]).wait()

    def sent(index, src, send_sem):
        part = src.at[pl.ds(0, (DEVS - 1) * 8)]
        pltpu.make_async_copy(part, part, send_sem.at[index]).wait()

    def forward(i, carry):
        c, n = i // 3, lax.rem(i, 3)

        @pl.when(n == 0)
        def _():
            make_table(c)

        @pl.when(i == 0)
        def _():
            loaded(7 * LT, 0)
            gf[120:128, :] = jnp.zeros((8, LON), f32)

        @pl.when((i == 1) | (i == 2))
        def _():
            loaded(6 * LT, 7 + i)

        @pl.when(i == 2)
        def _():
            for copy in small[1:]:
                copy.start()
            for s in range(SLOTS):
                pltpu.make_async_copy(
                    plm.at[s], pf.at[pl.ds(LAT * s, LAT)], load_sem.at[1]
                ).start()

        @pl.when(c == 0)
        def _():
            lax.fori_loop(8 * n, 8 * n + 8, split_grid, 0)

        forward_dft(c, n)

        @pl.when(i == 1)
        def _():
            pl.semaphore_wait(barrier, DEVS - 1)

        @pl.when(n > 0)
        def _():
            send(c, n - 1, s1, r1, send1, recv1)

        return carry

    lax.fori_loop(0, 6, forward, 0)

    pltpu.make_async_copy(pf, pf, load_sem.at[1]).wait()

    def split_plm(i, carry):
        rows = pl.ds(pl.multiple_of(64 * i, 64), 64)
        ph[rows, :], pw[rows, :] = split(pf[rows, :])
        return carry

    lax.fori_loop(0, SLOTS * LAT // 64, split_plm, 0)

    for copy in small[1:]:
        copy.wait()
    pad = PAD - LEVELS
    for i, part in enumerate(split(jnp.concatenate([min_v[...], jnp.zeros((pad, LEVELS), f32)], 0))):
        modes[i] = dot(part, order_v[...].astype(bf16), NN).astype(bf16)
    for i, part in enumerate(split(jnp.concatenate([mout_v[...], jnp.zeros((LEVELS, pad), f32)], 1))):
        modes[2 + i] = dot(order_tv[...].astype(bf16), part, NN).astype(bf16)
    eye = lax.broadcasted_iota(jnp.int32, (PAD, LEVELS), 0) == lax.broadcasted_iota(
        jnp.int32, (PAD, LEVELS), 1
    )
    damp[...] = jnp.sum(jnp.where(eye, damp_row[...], 0.0), axis=1, keepdims=True)
    x[LEVELS:PAD, :] = jnp.zeros((PAD - LEVELS, LAT), f32)
    lane8 = lanes(8)

    def middle(c, outer):
        arrive(2 * c, r1, recv1)
        arrive(2 * c + 1, r1, recv1)
        acc[...] = jnp.zeros((WAVES * 8, 128), f32)

        def slot(s, carry):
            base = HALF * c + 1 + s
            for k in range(16):
                tiles = [
                    pick(t, lambda p: r1[pl.ds(base + ((p - k) % 16) * 128 + 3 * t, 8, ROWS), :])
                    for t in range(MAIN)
                ]
                for t, value in enumerate(ring(tiles, LT * k)):
                    x[8 * k : 8 * k + 8, 128 * t : 128 * t + 128] = value
            tiles = [None] * MAIN
            for q in range(WAVES):
                own = r1[pl.ds(HALF * c + q * 128, 8, ROWS), :]
                own = pltpu.roll(own, lax.rem(LT * q - LT * s + 768, 128), 1)
                t, off = divmod(LT * q, 128)
                tiles[t] = own if off == 0 else jnp.where(lane8 < off, tiles[t], own)
                if off + LT > 128:
                    tiles[t + 1] = own
            for t in range(MAIN):
                x[128:136, 128 * t : 128 * t + 128] = tiles[t]

            prow = pl.ds(pl.multiple_of(LAT * s, LAT), LAT)
            xh, xl = split(x[...])
            spec = dot3(xh, xl, ph[prow, :], pw[prow, :], NN)
            degree = waves[SLOTS * me + s] + lax.broadcasted_iota(jnp.int32, (PAD, COEFF), 1)
            growth = (degree * (degree + 1)).astype(f32)
            factor = jnp.where(degree < COEFF, 1.0 / (1.0 + damp[...] * growth), 0.0)
            sh, sl = split(spec)
            modal = dot3(modes[0], modes[1], sh, sl, NN) * factor
            mh, ml = split(modal)
            solved = dot3(modes[2], modes[3], mh, ml, NN)
            vh, vl = split(solved)
            x[...] = dot3(vh, vl, ph[prow, :], pw[prow, :], NT)

            for k in range(16):
                tiles = [x[8 * k : 8 * k + 8, 128 * t : 128 * t + 128] for t in range(MAIN)]
                for t, value in enumerate(ring(tiles, -LT * k)):
                    e[8 * k : 8 * k + 8, 128 * t : 128 * t + 128] = value
            for q in range(WAVES):
                for t in range(MAIN):

                    def get(p):
                        k = (p - q) % 16
                        return e[8 * k : 8 * k + 8, 128 * t : 128 * t + 128]

                    s2[pl.ds(base + q * 128 + 3 * t, 8, ROWS), :] = pick(t, get)
                t, off = divmod(LT * q, 128)
                own = x[128:136, 128 * t : 128 * t + 128]
                if off + LT > 128:
                    after = x[128:136, 128 * t + 128 : 128 * t + 256]
                    own = jnp.where(lane8 < off, after, own)
                own = pltpu.roll(own, lax.rem(LT * s - LT * q + 768, 128), 1)
                inside = (lane8 >= LT * s) & (lane8 < LT * s + LT)
                acc[8 * q : 8 * q + 8, :] = jnp.where(inside, own, acc[8 * q : 8 * q + 8, :])
            return carry

        lax.fori_loop(0, SLOTS, slot, 0)
        s2[pl.ds(HALF * c, DEVS, ROWS), :] = acc[...]


        def out_half(h, carry):
            send(c, h, s2, r2, send2, recv2)
            return carry

        lax.fori_loop(0, 2, out_half, 0)
        return outer

    lax.fori_loop(0, 2, middle, 0)

    def returned(j, carry):
        c, h = j // 2, lax.rem(j, 2)
        rows = pl.ds(pl.multiple_of(384 * h, 128), 384)
        part = pl.ds(pl.multiple_of(384 * c, 128), 384)
        arrive(j, r2, recv2)

        for i in range(3):
            u = 3 * h + i
            rows_u = pl.ds(pl.multiple_of(128 * u, 128), 128)
            for s in range(SLOTS):
                start = jnp.where(u == 0, 0, 3 * u - 2 + s)
                tile = r2[pl.ds(HALF * c + start, DEVS, ROWS), :]
                if i == 0:
                    inside = (lane128 >= LT * s) & (lane128 < LT * s + LT)
                    tile = jnp.where(inside | (u > 0), tile, 0.0)
                cols_s = slice(128 * s, 128 * s + 128)
                rth[rows_u, cols_s], rtl[rows_u, cols_s] = split(tile.T)

        @pl.when(j < 3)
        def _():
            def adjoint(n, inner):
                cols = pl.ds(pl.multiple_of(256 * n, 256), 256)
                y = dot3_deep(rth[rows, :], rtl[rows, :], th[part, cols], tl[part, cols])
                gf[rows, cols] = jnp.where(c == 0, y, gf[rows, cols] + y)
                return inner

            lax.fori_loop(0, LON // 256, adjoint, 0)

        @pl.when(j == 2)
        def _():
            gf[0:40, :] = gf[0:40, :] + gf[40:80, :] + gf[80:120, :]
            for index in range(4):
                sent(index, s1, send1)
            for index in range(3):
                sent(index, s2, send2)

        return carry

    lax.fori_loop(0, 4, returned, 0)
    sent(3, s2, send2)


def finish(gf, th, tl, rth, rtl, out, rest, sem):
    w = lax.axis_index("wave")
    copies = []

    def write(src, dst, index):
        copy = pltpu.make_async_copy(src, dst, sem.at[index])
        copy.start()
        copies.append(copy)

    write(gf.at[pl.ds(0, LT)], out.at[16], 0)
    for p in range(6):
        write(gf.at[pl.ds(128 + LT * p, LT)], out.at[lax.rem(p - w + 16, 16)], 1 + p)
    rest[0:16, :] = gf[368:384, :]

    def step(n, carry):
        cols = pl.ds(pl.multiple_of(256 * n, 256), 256)
        rest[16:400, cols] = gf[384:768, cols] + dot3_deep(
            rth[384:768, :], rtl[384:768, :], th[384:768, cols], tl[384:768, cols]
        )
        for p in range(6, 16):
            pltpu.make_async_copy(
                rest.at[pl.ds(LT * (p - 6), LT), cols],
                out.at[lax.rem(p - w + 16, 16), :, cols],
                sem.at[7],
            ).start()
        return carry

    lax.fori_loop(0, LON // 256, step, 0)
    pltpu.make_async_copy(rest, rest, sem.at[7]).wait()
    for copy in copies:
        copy.wait()


def circle_table():
    wave = np.arange(DEVS * SLOTS)[:, None]
    near = 2.0 * math.pi / LON * (wave * np.arange(128)[None, :] % LON)
    far = 2.0 * math.pi / 10 * (wave * np.arange(16)[None, :] % 10)
    table = np.zeros((DEVS * SLOTS, 384))
    table[:, :128] = np.cos(near) / math.sqrt(LON)
    table[:, 128:256] = np.sin(near) / math.sqrt(LON)
    table[:, 256:272] = np.cos(far)
    table[:, 272:288] = np.sin(far)
    return table.astype(np.float32)


def level_order():
    matrix = np.zeros((LEVELS, PAD), np.float32)
    level = np.arange(LEVELS)
    matrix[level, level % LV * LEVS + level // LV] = 1
    return matrix


def local(grid_in, wavenumbers, legendre, modes_in, modes_out, damping):
    order = level_order()
    vmem = pl.BlockSpec(memory_space=pltpu.VMEM)
    hbm = pl.BlockSpec(memory_space=pl.ANY)
    dma = pltpu.SemaphoreType.DMA
    held = pl.pallas_call(
        kernel,
        out_shape=[
            pltpu.VMEM((768, LON), f32),
            pltpu.VMEM((768, LON), bf16),
            pltpu.VMEM((768, LON), bf16),
            pltpu.VMEM((768, 384), bf16),
            pltpu.VMEM((768, 384), bf16),
        ],
        in_specs=[pl.BlockSpec(memory_space=pltpu.SMEM), hbm, vmem] + [hbm] * 7,
        out_specs=[vmem] * 5,
        scratch_shapes=[
            pltpu.VMEM((768, LON), bf16),
            pltpu.VMEM((768, LON), bf16),
            pltpu.VMEM((SLOTS * LAT, COEFF), f32),
            pltpu.VMEM((SLOTS * LAT, COEFF), bf16),
            pltpu.VMEM((SLOTS * LAT, COEFF), bf16),
            pltpu.VMEM((2 * HALF, 128), f32),
            pltpu.VMEM((2 * HALF, 128), f32),
            pltpu.VMEM((2 * HALF, 128), f32),
            pltpu.VMEM((2 * HALF, 128), f32),
            pltpu.VMEM((PAD, LAT), f32),
            pltpu.VMEM((128, LAT), f32),
            pltpu.VMEM((WAVES * 8, 128), f32),
            pltpu.VMEM((4, PAD, PAD), bf16),
            pltpu.VMEM((PAD, 1), f32),
            pltpu.VMEM((DEVS * SLOTS, 384), f32),
            pltpu.VMEM((LEVELS, LEVELS), f32),
            pltpu.VMEM((LEVELS, LEVELS), f32),
            pltpu.VMEM((LEVELS, PAD), f32),
            pltpu.VMEM((PAD, LEVELS), f32),
            pltpu.VMEM((DEVS * SLOTS, 128), f32),
            pltpu.VMEM((DEVS * SLOTS, 128), f32),
            pltpu.VMEM((DEVS * SLOTS, 128), f32),
            pltpu.VMEM((1, DEVS * SLOTS), jnp.int32),
            dma((10,)),
            dma((4,)),
            dma((4,)),
            dma((4,)),
            dma((4,)),
        ],
        compiler_params=pltpu.CompilerParams(
            collective_id=0, has_side_effects=True, vmem_limit_bytes=48 << 20
        ),
        name="spectral_step",
    )(
        wavenumbers, wavenumbers, damping.reshape(1, -1), jnp.asarray(circle_table()),
        modes_in, modes_out, jnp.asarray(order), jnp.asarray(order.T.copy()),
        grid_in.reshape(LV, LT, LON), legendre,
    )
    result = pl.pallas_call(
        finish,
        out_shape=jax.ShapeDtypeStruct((LV, LT, LON), f32),
        in_specs=[vmem] * 5,
        out_specs=hbm,
        scratch_shapes=[
            pltpu.VMEM((400, LON), f32),
            dma((8,)),
        ],
        compiler_params=pltpu.CompilerParams(vmem_limit_bytes=40 << 20),
        name="finish",
    )(*[pltpu.with_memory_space_constraint(a, pltpu.VMEM) for a in held])
    return result.reshape(1, LV, LT, LON)


def solution(mesh):
    return jax.shard_map(
        local,
        mesh=mesh,
        in_specs=(P(None, "lev", "wave", None), P(), P(("wave", "lev"), None, None), P(), P(), P()),
        out_specs=P(None, "lev", "wave", None),
        check_vma=False,
    )
```

```python
import math

import jax
import jax.numpy as jnp
import numpy as np
from jax import lax
from jax.experimental import pallas as pl
from jax.experimental.pallas import tpu as pltpu
from jax.sharding import PartitionSpec as P

MESH = pl.DeviceIdType.MESH
f32 = jnp.float32
bf16 = jnp.bfloat16

LON = 1280
LAT = 640
COEFF = 640
WAVES = 16
LEVS = 8
DEVS = WAVES * LEVS
LV = 17
LT = 40
SLOTS = 3
LEVELS = LEVS * LV
PAD = 144
ROWS = 16
HALF = DEVS * ROWS
MAIN = 16 * LT // 128


def split(x):
    hi = x.astype(bf16)
    return hi, (x - hi.astype(f32)).astype(bf16)


def dot(a, b, dims):
    return lax.dot_general(a, b, (dims, ((), ())), preferred_element_type=f32)


TN = ((0,), (0,))
NN = ((1,), (0,))
NT = ((1,), (1,))


def dot3(ah, al, bh, bl, dims):
    rows = ah.shape[0]
    both = dot(jnp.concatenate([ah, al], 0), bh, dims)
    return both[:rows] + both[rows:] + dot(ah, bl, dims)


def dot3_deep(ah, al, bh, bl):
    return dot(jnp.concatenate([ah, al, ah], 1), jnp.concatenate([bh, bh, bl], 0), NN)


def lanes(rows):
    return lax.broadcasted_iota(jnp.int32, (rows, 128), 1)


def pick(tile, get):
    lane = lanes(8)
    value = None
    for p in range(128 * tile // LT, (128 * tile + 127) // LT + 1):
        value = get(p) if value is None else jnp.where(lane < LT * p - 128 * tile, value, get(p))
    return value


def ring(tiles, shift):
    whole, part = divmod(shift % (128 * MAIN), 128)
    if part == 0:
        return [tiles[(t + whole) % MAIN] for t in range(MAIN)]
    lane = lanes(8)
    rolled = [pltpu.roll(x, 128 - part, 1) for x in tiles]
    return [
        jnp.where(lane < 128 - part, rolled[(t + whole) % MAIN], rolled[(t + whole + 1) % MAIN])
        for t in range(MAIN)
    ]


def coordinates():
    w = lax.axis_index("wave")
    v = lax.axis_index("lev")
    return 2 * (v // 4) + w // 8, lax.rem(v, 4), lax.rem(w // 2, 4), lax.rem(w, 2)


def each_peer(visit):
    x, y, z, core = coordinates()
    xs = [lax.rem(x + a, 4) for a in range(4)]
    wave_x = [8 * lax.rem(a, 2) for a in xs]
    lev_x = [4 * (a // 2) for a in xs]
    lev_y = [lax.rem(y + b, 4) for b in range(4)]

    def outer(j, carry):
        wave_c = lax.rem(core + j // 4, 2)
        wave_z = [2 * lax.rem(z + j + d, 4) + wave_c for d in range(4)]
        for i in range(1, 16):
            a, b = i % 4, i // 4
            visit(wave_x[a] + wave_z[(b + 2 * a) % 4], lev_x[a] + lev_y[(a + b) % 4])
        return carry

    lax.fori_loop(0, 8, outer, 0)
    for j in range(1, 8):
        visit(wave_x[0] + 2 * lax.rem(z + j, 4) + lax.rem(core + j // 4, 2), lev_x[0] + lev_y[0])


def far_first():
    order = []
    for i in range(1, DEVS):
        a, b, d, core = i % 4, i // 4 % 4, i // 16 % 4, i // 64
        order.append((a, (a + b) % 4, (b + d + 2 * a) % 4, core))
    return sorted(order, key=lambda o: -sum(min(k, 4 - k) for k in o[:3]))


def each_peer_far_first(visit):
    x, y, z, core = coordinates()
    xs = [lax.rem(x + a, 4) for a in range(4)]
    wave_x = [8 * lax.rem(a, 2) for a in xs]
    lev_x = [4 * (a // 2) for a in xs]
    lev_y = [lax.rem(y + b, 4) for b in range(4)]
    wave_z = [2 * lax.rem(z + d, 4) for d in range(4)]
    wave_c = [core, 1 - core]
    for a, b, d, other in far_first():
        visit(wave_x[a] + wave_z[d] + wave_c[other], lev_x[a] + lev_y[b])


def kernel(
    waves, damp_all, circle, modes_in, modes_out, order, order_t, grid, plm,
    gf, th, tl, rth, rtl,
    gh, gl, pf, ph, pw, s1, r1, s2, r2, x, e, acc, modes, damp,
    circle_v, min_v, mout_v, order_v, order_tv, near_cos, near_sin, far, waves_row, damp_row,
    load_sem, send1, recv1, send2, recv2,
):
    w = lax.axis_index("wave")
    v = lax.axis_index("lev")
    me = w * LEVS + v

    barrier = pltpu.get_barrier_semaphore()

    def greet(to_wave, to_lev):
        pl.semaphore_signal(barrier, inc=1, device_id=(to_wave, to_lev), device_id_type=MESH)

    each_peer(greet)
    small = [
        pltpu.make_async_copy(a, b, load_sem.at[2 + i if i < 5 else 10])
        for i, (a, b) in enumerate(
            [
                (circle, circle_v), (modes_in, min_v), (modes_out, mout_v),
                (order, order_v), (order_t, order_tv), (damp_all, damp_row),
            ]
        )
    ]
    row_copy = pltpu.make_async_copy(waves, waves_row.at[0], load_sem.at[7])
    row_copy.start()
    small[0].start()
    for s in range(SLOTS):
        pltpu.make_async_copy(
            grid.at[16], gf.at[pl.ds(LT * s, LT)], load_sem.at[0]
        ).start()

    def load_level(p):
        pltpu.make_async_copy(
            grid.at[lax.rem(p - w + 16, 16)],
            gf.at[pl.ds(128 + LT * p, LT)],
            load_sem.at[0 if p < 4 else 7 + (p + 2) // 6],
        ).start()

    for p in range(4):
        load_level(p)

    for p in range(4, 16):
        load_level(p)

    slots = DEVS * SLOTS
    eye = lax.broadcasted_iota(jnp.int32, (slots, slots), 0) == lax.broadcasted_iota(
        jnp.int32, (slots, slots), 1
    )
    row_copy.wait()
    column = jnp.sum(
        jnp.where(eye, waves_row[...].astype(f32), 0.0), axis=1, keepdims=True
    ).astype(jnp.int32)
    chosen = (lax.broadcasted_iota(jnp.int32, (slots, slots), 1) == column).astype(bf16)
    small[0].wait()
    top, rest = split(circle_v[...])
    rows3 = dot(chosen, top, NN) + dot(chosen, rest, NN)
    near_cos[...] = rows3[:, 0:128]
    near_sin[...] = rows3[:, 128:256]
    far[...] = rows3[:, 256:384]

    def make_table(c):
        def table(s, carry):
            mine = pl.ds(s, DEVS, SLOTS)
            rows = pl.ds(pl.multiple_of(384 * c + DEVS * s, DEVS), DEVS)
            cosine, sine, f = near_cos[mine, :], near_sin[mine, :], far[mine, :]
            first = jnp.where(c == 0, cosine, -sine)
            second = jnp.where(c == 0, sine, cosine)
            for a in range(LON // 128):
                ca, sa = f[:, a : a + 1], f[:, 16 + a : 17 + a]
                col = slice(128 * a, 128 * a + 128)
                th[rows, col], tl[rows, col] = split(first * ca - second * sa)
            return carry

        lax.fori_loop(0, SLOTS, table, 0)

    def loaded(rows, index):
        part = gf.at[pl.ds(0, rows)]
        pltpu.make_async_copy(part, part, load_sem.at[index]).wait()

    def split_grid(i, carry):
        rows = pl.ds(pl.multiple_of(32 * i, 32), 32)
        gh[rows, :], gl[rows, :] = split(gf[rows, :])
        return carry

    lane128 = lanes(128)

    def forward_dft(c, n):
        cols = pl.ds(pl.multiple_of(256 * n, 256), 256)
        part = pl.ds(pl.multiple_of(384 * c, 128), 384)
        y = dot3(th[part, :], tl[part, :], gh[cols, :], gl[cols, :], NT)
        y0, y1 = y[:, 0:128], y[:, 128:256]

        @pl.when(n == 0)
        def _():
            last = jnp.where(
                lane128 < LT, y0[0:128], jnp.where(lane128 < 2 * LT, y0[128:256], y0[256:384])
            )
            s1[pl.ds(HALF * c, DEVS, ROWS), :] = last

        @pl.when(n > 0)
        def _():
            for s in range(SLOTS):
                s1[pl.ds(HALF * c + 6 * n - 2 + s, DEVS, ROWS), :] = y0[128 * s : 128 * s + 128]

        for s in range(SLOTS):
            s1[pl.ds(HALF * c + 6 * n + 1 + s, DEVS, ROWS), :] = y1[128 * s : 128 * s + 128]

    def send(c, h, src, dst, send_sem, recv_sem):
        send_rows(each_peer, c, 8 * h, 8, 2 * c + h, src, dst, send_sem, recv_sem)

    def send_rows(each, c, first, rows, index, src, dst, send_sem, recv_sem):

        def block(d):
            return pl.ds(pl.multiple_of((c * DEVS + d) * ROWS + first, rows), rows)

        pltpu.make_async_copy(src.at[block(me)], dst.at[block(me)], recv_sem.at[index]).start()

        def go(to_wave, to_lev):
            pltpu.make_async_remote_copy(
                src_ref=src.at[block(to_wave * LEVS + to_lev)],
                dst_ref=dst.at[block(me)],
                send_sem=send_sem.at[index],
                recv_sem=recv_sem.at[index],
                device_id=(to_wave, to_lev),
                device_id_type=MESH,
            ).start()

        each(go)

    def arrive(index, dst, recv_sem, rows=8):
        part = dst.at[pl.ds(0, DEVS * rows)]
        pltpu.make_async_copy(part, part, recv_sem.at[index]).wait()

    def sent(index, src, send_sem, rows=8):
        part = src.at[pl.ds(0, (DEVS - 1) * rows)]
        pltpu.make_async_copy(part, part, send_sem.at[index]).wait()

    def forward(i, carry):
        c, n = i // 3, lax.rem(i, 3)

        @pl.when(n == 0)
        def _():
            make_table(c)

        @pl.when(i == 0)
        def _():
            loaded(7 * LT, 0)
            gf[120:128, :] = jnp.zeros((8, LON), f32)

        @pl.when((i == 1) | (i == 2))
        def _():
            loaded(6 * LT, 7 + i)

        @pl.when(i == 2)
        def _():
            for copy in small[1:]:
                copy.start()
            for s in range(SLOTS):
                pltpu.make_async_copy(
                    plm.at[s], pf.at[pl.ds(LAT * s, LAT)], load_sem.at[1]
                ).start()

        @pl.when(c == 0)
        def _():
            lax.fori_loop(8 * n, 8 * n + 8, split_grid, 0)

        forward_dft(c, n)

        @pl.when(i == 0)
        def _():
            pl.semaphore_wait(barrier, DEVS - 1)

        @pl.when(i < 2)
        def _():
            send_rows(each_peer, 0, 4 * i, 4, 4 * i, s1, r1, send1, recv1)

        @pl.when((n > 0) & (i != 1))
        def _():
            send(c, n - 1, s1, r1, send1, recv1)

        return carry

    lax.fori_loop(0, 6, forward, 0)

    pltpu.make_async_copy(pf, pf, load_sem.at[1]).wait()

    def split_plm(i, carry):
        rows = pl.ds(pl.multiple_of(64 * i, 64), 64)
        ph[rows, :], pw[rows, :] = split(pf[rows, :])
        return carry

    lax.fori_loop(0, SLOTS * LAT // 64, split_plm, 0)

    for copy in small[1:]:
        copy.wait()
    pad = PAD - LEVELS
    for i, part in enumerate(split(jnp.concatenate([min_v[...], jnp.zeros((pad, LEVELS), f32)], 0))):
        modes[i] = dot(part, order_v[...].astype(bf16), NN).astype(bf16)
    for i, part in enumerate(split(jnp.concatenate([mout_v[...], jnp.zeros((LEVELS, pad), f32)], 1))):
        modes[2 + i] = dot(order_tv[...].astype(bf16), part, NN).astype(bf16)
    eye = lax.broadcasted_iota(jnp.int32, (PAD, LEVELS), 0) == lax.broadcasted_iota(
        jnp.int32, (PAD, LEVELS), 1
    )
    damp[...] = jnp.sum(jnp.where(eye, damp_row[...], 0.0), axis=1, keepdims=True)
    x[LEVELS:PAD, :] = jnp.zeros((PAD - LEVELS, LAT), f32)
    lane8 = lanes(8)

    def middle(c, outer):
        @pl.when(c == 0)
        def _():
            arrive(0, r1, recv1, 4)
            arrive(4, r1, recv1, 4)

        @pl.when(c == 1)
        def _():
            arrive(2, r1, recv1)

        arrive(2 * c + 1, r1, recv1)
        acc[...] = jnp.zeros((WAVES * 8, 128), f32)

        def slot(s, carry):
            base = HALF * c + 1 + s
            for k in range(16):
                tiles = [
                    pick(t, lambda p: r1[pl.ds(base + ((p - k) % 16) * 128 + 3 * t, 8, ROWS), :])
                    for t in range(MAIN)
                ]
                for t, value in enumerate(ring(tiles, LT * k)):
                    x[8 * k : 8 * k + 8, 128 * t : 128 * t + 128] = value
            tiles = [None] * MAIN
            for q in range(WAVES):
                own = r1[pl.ds(HALF * c + q * 128, 8, ROWS), :]
                own = pltpu.roll(own, lax.rem(LT * q - LT * s + 768, 128), 1)
                t, off = divmod(LT * q, 128)
                tiles[t] = own if off == 0 else jnp.where(lane8 < off, tiles[t], own)
                if off + LT > 128:
                    tiles[t + 1] = own
            for t in range(MAIN):
                x[128:136, 128 * t : 128 * t + 128] = tiles[t]

            prow = pl.ds(pl.multiple_of(LAT * s, LAT), LAT)
            xh, xl = split(x[...])
            spec = dot3(xh, xl, ph[prow, :], pw[prow, :], NN)
            here = lax.broadcasted_iota(jnp.int32, (1, slots), 1) == SLOTS * me + s
            wave = jnp.sum(
                jnp.where(here, waves_row[...].astype(f32), 0.0), axis=1, keepdims=True
            ).astype(jnp.int32)
            degree = wave + lax.broadcasted_iota(jnp.int32, (PAD, COEFF), 1)
            growth = (degree * (degree + 1)).astype(f32)
            factor = jnp.where(degree < COEFF, 1.0 / (1.0 + damp[...] * growth), 0.0)
            sh, sl = split(spec)
            modal = dot3(modes[0], modes[1], sh, sl, NN) * factor
            mh, ml = split(modal)
            solved = dot3(modes[2], modes[3], mh, ml, NN)
            vh, vl = split(solved)
            x[...] = dot3(vh, vl, ph[prow, :], pw[prow, :], NT)

            for k in range(16):
                tiles = [x[8 * k : 8 * k + 8, 128 * t : 128 * t + 128] for t in range(MAIN)]
                for t, value in enumerate(ring(tiles, -LT * k)):
                    e[8 * k : 8 * k + 8, 128 * t : 128 * t + 128] = value
            for q in range(WAVES):
                for t in range(MAIN):

                    def get(p):
                        k = (p - q) % 16
                        return e[8 * k : 8 * k + 8, 128 * t : 128 * t + 128]

                    s2[pl.ds(base + q * 128 + 3 * t, 8, ROWS), :] = pick(t, get)
                t, off = divmod(LT * q, 128)
                own = x[128:136, 128 * t : 128 * t + 128]
                if off + LT > 128:
                    after = x[128:136, 128 * t + 128 : 128 * t + 256]
                    own = jnp.where(lane8 < off, after, own)
                own = pltpu.roll(own, lax.rem(LT * s - LT * q + 768, 128), 1)
                inside = (lane8 >= LT * s) & (lane8 < LT * s + LT)
                acc[8 * q : 8 * q + 8, :] = jnp.where(inside, own, acc[8 * q : 8 * q + 8, :])
            return carry

        lax.fori_loop(0, SLOTS, slot, 0)
        s2[pl.ds(HALF * c, DEVS, ROWS), :] = acc[...]


        def out_half(h, carry):
            @pl.when((c == 0) | (h == 0))
            def _():
                send_rows(
                    each_peer_far_first, c, 8 * h, 8, 2 * c + h, s2, r2, send2, recv2
                )

            @pl.when((c == 1) & (h > 0))
            def _():
                send_rows(
                    each_peer_far_first, c, 4 + 4 * h, 4, 2 + h, s2, r2, send2, recv2
                )

            return carry

        lax.fori_loop(0, 2 + c, out_half, 0)
        return outer

    lax.fori_loop(0, 2, middle, 0)

    def transpose(c, u, s):
        start = jnp.where(u == 0, 0, 3 * u - 2 + s)
        tile = r2[pl.ds(HALF * c + start, DEVS, ROWS), :]
        inside = (lane128 >= LT * s) & (lane128 < LT * s + LT)
        tile = jnp.where(inside | (u > 0), tile, 0.0)
        rows_u = pl.ds(pl.multiple_of(128 * u, 128), 128)
        cols_s = slice(128 * s, 128 * s + 128)
        rth[rows_u, cols_s], rtl[rows_u, cols_s] = split(tile.T)

    def returned(j, carry):
        c, h = j // 2, lax.rem(j, 2)
        rows = pl.ds(pl.multiple_of(384 * h, 128), 384)
        part = pl.ds(pl.multiple_of(384 * c, 128), 384)
        arrive(j, r2, recv2)
        for i in range(3):
            for s in range(SLOTS):
                transpose(c, 3 * h + i, s)

        def adjoint(n, inner):
            cols = pl.ds(pl.multiple_of(256 * n, 256), 256)
            y = dot3_deep(rth[rows, :], rtl[rows, :], th[part, cols], tl[part, cols])
            gf[rows, cols] = jnp.where(c == 0, y, gf[rows, cols] + y)
            return inner

        lax.fori_loop(0, LON // 256, adjoint, 0)
        return carry

    lax.fori_loop(0, 3, returned, 0)
    gf[0:40, :] = gf[0:40, :] + gf[40:80, :] + gf[80:120, :]
    for index in range(1, 4):
        sent(index, s1, send1)
    sent(0, s1, send1, 4)
    sent(4, s1, send1, 4)
    for index in range(3):
        sent(index, s2, send2)
    arrive(3, r2, recv2, 4)
    for u, s in ((3, 0), (3, 1), (3, 2), (4, 0), (4, 1)):
        transpose(1, u, s)

    def adjoint_tile(n, carry):
        cols = pl.ds(pl.multiple_of(256 * n, 256), 256)
        gf[384:512, cols] += dot3_deep(
            rth[384:512, :], rtl[384:512, :], th[384:768, cols], tl[384:768, cols]
        )
        return carry

    lax.fori_loop(0, LON // 256, adjoint_tile, 0)
    sent(3, s2, send2, 4)
    arrive(4, r2, recv2, 4)
    for u, s in ((4, 2), (5, 0), (5, 1), (5, 2)):
        transpose(1, u, s)
    sent(4, s2, send2, 4)


def finish(gf, th, tl, rth, rtl, out, rest, sem):
    w = lax.axis_index("wave")
    copies = []

    def write(src, dst, index):
        copy = pltpu.make_async_copy(src, dst, sem.at[index])
        copy.start()
        copies.append(copy)

    write(gf.at[pl.ds(0, LT)], out.at[16], 0)
    for p in range(9):
        write(gf.at[pl.ds(128 + LT * p, LT)], out.at[lax.rem(p - w + 16, 16)], 1 + p)
    rest[0:24, :] = gf[488:512, :]

    def step(n, carry):
        cols = pl.ds(pl.multiple_of(256 * n, 256), 256)
        rest[24:280, cols] = gf[512:768, cols] + dot3_deep(
            rth[512:768, :], rtl[512:768, :], th[384:768, cols], tl[384:768, cols]
        )
        for p in range(9, 16):
            pltpu.make_async_copy(
                rest.at[pl.ds(LT * (p - 9), LT), cols],
                out.at[lax.rem(p - w + 16, 16), :, cols],
                sem.at[10],
            ).start()
        return carry

    lax.fori_loop(0, LON // 256, step, 0)
    pltpu.make_async_copy(rest, rest, sem.at[10]).wait()
    for copy in copies:
        copy.wait()


def circle_table():
    wave = np.arange(DEVS * SLOTS)[:, None]
    near = 2.0 * math.pi / LON * (wave * np.arange(128)[None, :] % LON)
    far = 2.0 * math.pi / 10 * (wave * np.arange(16)[None, :] % 10)
    table = np.zeros((DEVS * SLOTS, 384))
    table[:, :128] = np.cos(near) / math.sqrt(LON)
    table[:, 128:256] = np.sin(near) / math.sqrt(LON)
    table[:, 256:272] = np.cos(far)
    table[:, 272:288] = np.sin(far)
    return table.astype(np.float32)


def level_order():
    matrix = np.zeros((LEVELS, PAD), np.float32)
    level = np.arange(LEVELS)
    matrix[level, level % LV * LEVS + level // LV] = 1
    return matrix


def local(grid_in, wavenumbers, legendre, modes_in, modes_out, damping):
    order = level_order()
    vmem = pl.BlockSpec(memory_space=pltpu.VMEM)
    hbm = pl.BlockSpec(memory_space=pl.ANY)
    dma = pltpu.SemaphoreType.DMA
    held = pl.pallas_call(
        kernel,
        out_shape=[
            pltpu.VMEM((768, LON), f32),
            pltpu.VMEM((768, LON), bf16),
            pltpu.VMEM((768, LON), bf16),
            pltpu.VMEM((768, 384), bf16),
            pltpu.VMEM((768, 384), bf16),
        ],
        in_specs=[hbm] * 9,
        out_specs=[vmem] * 5,
        scratch_shapes=[
            pltpu.VMEM((768, LON), bf16),
            pltpu.VMEM((768, LON), bf16),
            pltpu.VMEM((SLOTS * LAT, COEFF), f32),
            pltpu.VMEM((SLOTS * LAT, COEFF), bf16),
            pltpu.VMEM((SLOTS * LAT, COEFF), bf16),
            pltpu.VMEM((2 * HALF, 128), f32),
            pltpu.VMEM((2 * HALF, 128), f32),
            pltpu.VMEM((2 * HALF, 128), f32),
            pltpu.VMEM((2 * HALF, 128), f32),
            pltpu.VMEM((PAD, LAT), f32),
            pltpu.VMEM((128, LAT), f32),
            pltpu.VMEM((WAVES * 8, 128), f32),
            pltpu.VMEM((4, PAD, PAD), bf16),
            pltpu.VMEM((PAD, 1), f32),
            pltpu.VMEM((DEVS * SLOTS, 384), f32),
            pltpu.VMEM((LEVELS, LEVELS), f32),
            pltpu.VMEM((LEVELS, LEVELS), f32),
            pltpu.VMEM((LEVELS, PAD), f32),
            pltpu.VMEM((PAD, LEVELS), f32),
            pltpu.VMEM((DEVS * SLOTS, 128), f32),
            pltpu.VMEM((DEVS * SLOTS, 128), f32),
            pltpu.VMEM((DEVS * SLOTS, 128), f32),
            pltpu.VMEM((1, DEVS * SLOTS), jnp.int32),
            pltpu.VMEM((1, LEVELS), f32),
            dma((11,)),
            dma((5,)),
            dma((5,)),
            dma((5,)),
            dma((5,)),
        ],
        compiler_params=pltpu.CompilerParams(
            collective_id=0, has_side_effects=True, vmem_limit_bytes=48 << 20
        ),
        name="spectral_step",
    )(
        wavenumbers, damping.reshape(1, -1), jnp.asarray(circle_table()),
        modes_in, modes_out, jnp.asarray(order), jnp.asarray(order.T.copy()),
        grid_in.reshape(LV, LT, LON), legendre,
    )
    result = pl.pallas_call(
        finish,
        out_shape=jax.ShapeDtypeStruct((LV, LT, LON), f32),
        in_specs=[vmem] * 5,
        out_specs=hbm,
        scratch_shapes=[
            pltpu.VMEM((280, LON), f32),
            dma((11,)),
        ],
        compiler_params=pltpu.CompilerParams(vmem_limit_bytes=40 << 20),
        name="finish",
    )(*[pltpu.with_memory_space_constraint(a, pltpu.VMEM) for a in held])
    return result.reshape(1, LV, LT, LON)


def solution(mesh):
    return jax.shard_map(
        local,
        mesh=mesh,
        in_specs=(P(None, "lev", "wave", None), P(), P(("wave", "lev"), None, None), P(), P(), P()),
        out_specs=P(None, "lev", "wave", None),
        check_vma=False,
    )
```

```python
import math

import jax
import jax.numpy as jnp
import numpy as np
from jax import lax
from jax.experimental import pallas as pl
from jax.experimental.pallas import tpu as pltpu
from jax.sharding import PartitionSpec as P

MESH = pl.DeviceIdType.MESH
f32 = jnp.float32
bf16 = jnp.bfloat16

LON = 1280
LAT = 640
COEFF = 640
WAVES = 16
LEVS = 8
DEVS = WAVES * LEVS
LV = 17
LT = 40
SLOTS = 3
LEVELS = LEVS * LV
PAD = 144
ROWS = 16
HALF = DEVS * ROWS
MAIN = 16 * LT // 128


def split(x):
    hi = x.astype(bf16)
    return hi, (x - hi.astype(f32)).astype(bf16)


def dot(a, b, dims):
    return lax.dot_general(a, b, (dims, ((), ())), preferred_element_type=f32)


TN = ((0,), (0,))
NN = ((1,), (0,))
NT = ((1,), (1,))


def dot3(ah, al, bh, bl, dims):
    rows = ah.shape[0]
    both = dot(jnp.concatenate([ah, al], 0), bh, dims)
    return both[:rows] + both[rows:] + dot(ah, bl, dims)


def dot3_deep(ah, al, bh, bl):
    return dot(jnp.concatenate([ah, al, ah], 1), jnp.concatenate([bh, bh, bl], 0), NN)


def lanes(rows):
    return lax.broadcasted_iota(jnp.int32, (rows, 128), 1)


def pick(tile, get):
    lane = lanes(8)
    value = None
    for p in range(128 * tile // LT, (128 * tile + 127) // LT + 1):
        value = get(p) if value is None else jnp.where(lane < LT * p - 128 * tile, value, get(p))
    return value


def ring(tiles, shift):
    whole, part = divmod(shift % (128 * MAIN), 128)
    if part == 0:
        return [tiles[(t + whole) % MAIN] for t in range(MAIN)]
    lane = lanes(8)
    rolled = [pltpu.roll(x, 128 - part, 1) for x in tiles]
    return [
        jnp.where(lane < 128 - part, rolled[(t + whole) % MAIN], rolled[(t + whole + 1) % MAIN])
        for t in range(MAIN)
    ]


def coordinates():
    w = lax.axis_index("wave")
    v = lax.axis_index("lev")
    return 2 * (v // 4) + w // 8, lax.rem(v, 4), lax.rem(w // 2, 4), lax.rem(w, 2)


def each_peer(visit):
    x, y, z, core = coordinates()
    xs = [lax.rem(x + a, 4) for a in range(4)]
    wave_x = [8 * lax.rem(a, 2) for a in xs]
    lev_x = [4 * (a // 2) for a in xs]
    lev_y = [lax.rem(y + b, 4) for b in range(4)]

    def outer(j, carry):
        wave_c = lax.rem(core + j // 4, 2)
        wave_z = [2 * lax.rem(z + j + d, 4) + wave_c for d in range(4)]
        for i in range(1, 16):
            a, b = i % 4, i // 4
            visit(wave_x[a] + wave_z[(b + 2 * a) % 4], lev_x[a] + lev_y[(a + b) % 4])
        return carry

    lax.fori_loop(0, 8, outer, 0)
    for j in range(1, 8):
        visit(wave_x[0] + 2 * lax.rem(z + j, 4) + lax.rem(core + j // 4, 2), lev_x[0] + lev_y[0])


def far_first():
    order = []
    for i in range(1, DEVS):
        a, b, d, core = i % 4, i // 4 % 4, i // 16 % 4, i // 64
        order.append((a, (a + b) % 4, (b + d + 2 * a) % 4, core))
    return sorted(order, key=lambda o: -sum(min(k, 4 - k) for k in o[:3]))


def each_peer_far_first(visit):
    x, y, z, core = coordinates()
    xs = [lax.rem(x + a, 4) for a in range(4)]
    wave_x = [8 * lax.rem(a, 2) for a in xs]
    lev_x = [4 * (a // 2) for a in xs]
    lev_y = [lax.rem(y + b, 4) for b in range(4)]
    wave_z = [2 * lax.rem(z + d, 4) for d in range(4)]
    wave_c = [core, 1 - core]
    for a, b, d, other in far_first():
        visit(wave_x[a] + wave_z[d] + wave_c[other], lev_x[a] + lev_y[b])


def kernel(
    waves, damp_all, circle, modes_in, modes_out, order, order_t, grid, plm,
    gf, th, tl, rth, rtl,
    gh, gl, pf, ph, pw, s1, r1, s2, r2, x, e, acc, modes, damp,
    circle_v, min_v, mout_v, order_v, order_tv, near_cos, near_sin, far, waves_row, damp_row,
    load_sem, send1, recv1, send2, recv2,
):
    w = lax.axis_index("wave")
    v = lax.axis_index("lev")
    me = w * LEVS + v

    barrier = pltpu.get_barrier_semaphore()

    def greet(to_wave, to_lev):
        pl.semaphore_signal(barrier, inc=1, device_id=(to_wave, to_lev), device_id_type=MESH)

    each_peer(greet)
    small = [
        pltpu.make_async_copy(a, b, load_sem.at[2 + i if i < 5 else 10])
        for i, (a, b) in enumerate(
            [
                (circle, circle_v), (modes_in, min_v), (modes_out, mout_v),
                (order, order_v), (order_t, order_tv), (damp_all, damp_row),
            ]
        )
    ]
    row_copy = pltpu.make_async_copy(waves, waves_row.at[0], load_sem.at[7])
    row_copy.start()
    small[0].start()
    for s in range(SLOTS):
        pltpu.make_async_copy(
            grid.at[16], gf.at[pl.ds(LT * s, LT)], load_sem.at[0]
        ).start()

    def load_level(p):
        pltpu.make_async_copy(
            grid.at[lax.rem(p - w + 16, 16)],
            gf.at[pl.ds(128 + LT * p, LT)],
            load_sem.at[0 if p < 4 else 7 + (p + 2) // 6],
        ).start()

    for p in range(4):
        load_level(p)

    for p in range(4, 16):
        load_level(p)

    slots = DEVS * SLOTS
    eye = lax.broadcasted_iota(jnp.int32, (slots, slots), 0) == lax.broadcasted_iota(
        jnp.int32, (slots, slots), 1
    )
    row_copy.wait()
    column = jnp.sum(
        jnp.where(eye, waves_row[...].astype(f32), 0.0), axis=1, keepdims=True
    ).astype(jnp.int32)
    chosen = (lax.broadcasted_iota(jnp.int32, (slots, slots), 1) == column).astype(bf16)
    small[0].wait()
    top, rest = split(circle_v[...])
    rows3 = dot(chosen, top, NN) + dot(chosen, rest, NN)
    near_cos[0:slots, :] = rows3[:, 0:128]
    near_sin[0:slots, :] = rows3[:, 128:256]
    far[0:slots, :] = rows3[:, 256:384]

    def make_table(c):
        def table(s, carry):
            mine = pl.ds(s, DEVS, SLOTS)
            rows = pl.ds(pl.multiple_of(384 * c + DEVS * s, DEVS), DEVS)
            cosine, sine, f = near_cos[mine, :], near_sin[mine, :], far[mine, :]
            first = jnp.where(c == 0, cosine, -sine)
            second = jnp.where(c == 0, sine, cosine)
            for a in range(LON // 128):
                ca, sa = f[:, a : a + 1], f[:, 16 + a : 17 + a]
                col = slice(128 * a, 128 * a + 128)
                th[rows, col], tl[rows, col] = split(first * ca - second * sa)
            return carry

        lax.fori_loop(0, SLOTS, table, 0)

    def loaded(rows, index):
        part = gf.at[pl.ds(0, rows)]
        pltpu.make_async_copy(part, part, load_sem.at[index]).wait()

    def split_grid(i, carry):
        rows = pl.ds(pl.multiple_of(32 * i, 32), 32)
        gh[rows, :], gl[rows, :] = split(gf[rows, :])
        return carry

    lane128 = lanes(128)

    def forward_dft(c, n):
        cols = pl.ds(pl.multiple_of(256 * n, 256), 256)
        part = pl.ds(pl.multiple_of(384 * c, 128), 384)
        y = dot3(th[part, :], tl[part, :], gh[cols, :], gl[cols, :], NT)
        y0, y1 = y[:, 0:128], y[:, 128:256]

        @pl.when(n == 0)
        def _():
            last = jnp.where(
                lane128 < LT, y0[0:128], jnp.where(lane128 < 2 * LT, y0[128:256], y0[256:384])
            )
            s1[pl.ds(HALF * c, DEVS, ROWS), :] = last

        @pl.when(n > 0)
        def _():
            for s in range(SLOTS):
                s1[pl.ds(HALF * c + 6 * n - 2 + s, DEVS, ROWS), :] = y0[128 * s : 128 * s + 128]

        for s in range(SLOTS):
            s1[pl.ds(HALF * c + 6 * n + 1 + s, DEVS, ROWS), :] = y1[128 * s : 128 * s + 128]

    def send(c, h, src, dst, send_sem, recv_sem):
        send_rows(each_peer, c, 8 * h, 8, 2 * c + h, src, dst, send_sem, recv_sem)

    def send_rows(each, c, first, rows, index, src, dst, send_sem, recv_sem):

        def block(d):
            return pl.ds(pl.multiple_of((c * DEVS + d) * ROWS + first, rows), rows)

        pltpu.make_async_copy(src.at[block(me)], dst.at[block(me)], recv_sem.at[index]).start()

        def go(to_wave, to_lev):
            pltpu.make_async_remote_copy(
                src_ref=src.at[block(to_wave * LEVS + to_lev)],
                dst_ref=dst.at[block(me)],
                send_sem=send_sem.at[index],
                recv_sem=recv_sem.at[index],
                device_id=(to_wave, to_lev),
                device_id_type=MESH,
            ).start()

        each(go)

    def arrive(index, dst, recv_sem, rows=8):
        part = dst.at[pl.ds(0, DEVS * rows)]
        pltpu.make_async_copy(part, part, recv_sem.at[index]).wait()

    def sent(index, src, send_sem, rows=8):
        part = src.at[pl.ds(0, (DEVS - 1) * rows)]
        pltpu.make_async_copy(part, part, send_sem.at[index]).wait()

    def forward(i, carry):
        c, n = i // 3, lax.rem(i, 3)

        @pl.when(n == 0)
        def _():
            make_table(c)

        @pl.when(i == 0)
        def _():
            loaded(7 * LT, 0)
            gf[120:128, :] = jnp.zeros((8, LON), f32)

        @pl.when((i == 1) | (i == 2))
        def _():
            loaded(6 * LT, 7 + i)

        @pl.when(i == 2)
        def _():
            for copy in small[1:]:
                copy.start()
            for s in range(SLOTS):
                pltpu.make_async_copy(
                    plm.at[s], pf.at[pl.ds(LAT * s, LAT)], load_sem.at[1]
                ).start()

        @pl.when(c == 0)
        def _():
            lax.fori_loop(8 * n, 8 * n + 8, split_grid, 0)

        forward_dft(c, n)

        @pl.when(i == 0)
        def _():
            pl.semaphore_wait(barrier, DEVS - 1)

        @pl.when(i < 2)
        def _():
            send_rows(each_peer, 0, 4 * i, 4, 4 * i, s1, r1, send1, recv1)

        @pl.when((n > 0) & (i != 1))
        def _():
            send(c, n - 1, s1, r1, send1, recv1)

        return carry

    lax.fori_loop(0, 6, forward, 0)

    pltpu.make_async_copy(pf, pf, load_sem.at[1]).wait()

    def split_plm(i, carry):
        rows = pl.ds(pl.multiple_of(64 * i, 64), 64)
        ph[rows, :], pw[rows, :] = split(pf[rows, :])
        return carry

    lax.fori_loop(0, SLOTS * LAT // 64, split_plm, 0)

    for copy in small[1:]:
        copy.wait()
    pad = PAD - LEVELS
    for i, part in enumerate(split(jnp.concatenate([min_v[...], jnp.zeros((pad, LEVELS), f32)], 0))):
        modes[i] = dot(part, order_v[...].astype(bf16), NN).astype(bf16)
    for i, part in enumerate(split(jnp.concatenate([mout_v[...], jnp.zeros((LEVELS, pad), f32)], 1))):
        modes[2 + i] = dot(order_tv[...].astype(bf16), part, NN).astype(bf16)
    eye = lax.broadcasted_iota(jnp.int32, (PAD, LEVELS), 0) == lax.broadcasted_iota(
        jnp.int32, (PAD, LEVELS), 1
    )
    damp[...] = jnp.sum(jnp.where(eye, damp_row[...], 0.0), axis=1, keepdims=True)
    x[LEVELS:PAD, :] = jnp.zeros((PAD - LEVELS, LAT), f32)
    lane8 = lanes(8)

    def middle(c, outer):
        @pl.when(c == 0)
        def _():
            arrive(0, r1, recv1, 4)
            arrive(4, r1, recv1, 4)

        @pl.when(c == 1)
        def _():
            arrive(2, r1, recv1)

        arrive(2 * c + 1, r1, recv1)
        acc[...] = jnp.zeros((WAVES * 8, 128), f32)

        def slot(s, carry):
            base = HALF * c + 1 + s
            for k in range(16):
                tiles = [
                    pick(t, lambda p: r1[pl.ds(base + ((p - k) % 16) * 128 + 3 * t, 8, ROWS), :])
                    for t in range(MAIN)
                ]
                for t, value in enumerate(ring(tiles, LT * k)):
                    x[8 * k : 8 * k + 8, 128 * t : 128 * t + 128] = value
            tiles = [None] * MAIN
            for q in range(WAVES):
                own = r1[pl.ds(HALF * c + q * 128, 8, ROWS), :]
                own = pltpu.roll(own, lax.rem(LT * q - LT * s + 768, 128), 1)
                t, off = divmod(LT * q, 128)
                tiles[t] = own if off == 0 else jnp.where(lane8 < off, tiles[t], own)
                if off + LT > 128:
                    tiles[t + 1] = own
            for t in range(MAIN):
                x[128:136, 128 * t : 128 * t + 128] = tiles[t]

            prow = pl.ds(pl.multiple_of(LAT * s, LAT), LAT)
            xh, xl = split(x[...])
            spec = dot3(xh, xl, ph[prow, :], pw[prow, :], NN)
            here = lax.broadcasted_iota(jnp.int32, (1, slots), 1) == SLOTS * me + s
            wave = jnp.sum(
                jnp.where(here, waves_row[...].astype(f32), 0.0), axis=1, keepdims=True
            ).astype(jnp.int32)
            degree = wave + lax.broadcasted_iota(jnp.int32, (PAD, COEFF), 1)
            growth = (degree * (degree + 1)).astype(f32)
            factor = jnp.where(degree < COEFF, 1.0 / (1.0 + damp[...] * growth), 0.0)
            sh, sl = split(spec)
            modal = dot3(modes[0], modes[1], sh, sl, NN) * factor
            mh, ml = split(modal)
            solved = dot3(modes[2], modes[3], mh, ml, NN)
            vh, vl = split(solved)
            x[...] = dot3(vh, vl, ph[prow, :], pw[prow, :], NT)

            for k in range(16):
                tiles = [x[8 * k : 8 * k + 8, 128 * t : 128 * t + 128] for t in range(MAIN)]
                for t, value in enumerate(ring(tiles, -LT * k)):
                    e[8 * k : 8 * k + 8, 128 * t : 128 * t + 128] = value
            for q in range(WAVES):
                for t in range(MAIN):

                    def get(p):
                        k = (p - q) % 16
                        return e[8 * k : 8 * k + 8, 128 * t : 128 * t + 128]

                    s2[pl.ds(base + q * 128 + 3 * t, 8, ROWS), :] = pick(t, get)
                t, off = divmod(LT * q, 128)
                own = x[128:136, 128 * t : 128 * t + 128]
                if off + LT > 128:
                    after = x[128:136, 128 * t + 128 : 128 * t + 256]
                    own = jnp.where(lane8 < off, after, own)
                own = pltpu.roll(own, lax.rem(LT * s - LT * q + 768, 128), 1)
                inside = (lane8 >= LT * s) & (lane8 < LT * s + LT)
                acc[8 * q : 8 * q + 8, :] = jnp.where(inside, own, acc[8 * q : 8 * q + 8, :])
            return carry

        lax.fori_loop(0, SLOTS, slot, 0)
        s2[pl.ds(HALF * c, DEVS, ROWS), :] = acc[...]


        def out_half(h, carry):
            @pl.when((c == 0) | (h == 0))
            def _():
                send_rows(
                    each_peer_far_first, c, 8 * h, 8, 2 * c + h, s2, r2, send2, recv2
                )

            @pl.when((c == 1) & (h > 0))
            def _():
                send_rows(
                    each_peer_far_first, c, 4 + 4 * h, 4, 2 + h, s2, r2, send2, recv2
                )

            return carry

        lax.fori_loop(0, 2 + c, out_half, 0)
        return outer

    lax.fori_loop(0, 2, middle, 0)

    def transpose(c, u, s):
        start = jnp.where(u == 0, 0, 3 * u - 2 + s)
        tile = r2[pl.ds(HALF * c + start, DEVS, ROWS), :]
        inside = (lane128 >= LT * s) & (lane128 < LT * s + LT)
        tile = jnp.where(inside | (u > 0), tile, 0.0)
        rows_u = pl.ds(pl.multiple_of(128 * u, 128), 128)
        cols_s = slice(128 * s, 128 * s + 128)
        rth[rows_u, cols_s], rtl[rows_u, cols_s] = split(tile.T)

    def returned(j, carry):
        c, h = j // 2, lax.rem(j, 2)
        rows = pl.ds(pl.multiple_of(384 * h, 128), 384)
        part = pl.ds(pl.multiple_of(384 * c, 128), 384)
        arrive(j, r2, recv2)
        for i in range(3):
            for s in range(SLOTS):
                transpose(c, 3 * h + i, s)

        def adjoint(n, inner):
            cols = pl.ds(pl.multiple_of(256 * n, 256), 256)
            y = dot3_deep(rth[rows, :], rtl[rows, :], th[part, cols], tl[part, cols])
            gf[rows, cols] = jnp.where(c == 0, y, gf[rows, cols] + y)
            return inner

        lax.fori_loop(0, LON // 256, adjoint, 0)
        return carry

    lax.fori_loop(0, 3, returned, 0)
    gf[0:40, :] = gf[0:40, :] + gf[40:80, :] + gf[80:120, :]
    for index in range(1, 4):
        sent(index, s1, send1)
    sent(0, s1, send1, 4)
    sent(4, s1, send1, 4)
    for index in range(3):
        sent(index, s2, send2)
    arrive(3, r2, recv2, 4)
    for u, s in ((3, 0), (3, 1), (3, 2), (4, 0), (4, 1)):
        transpose(1, u, s)

    def adjoint_tile(n, carry):
        cols = pl.ds(pl.multiple_of(256 * n, 256), 256)
        gf[384:512, cols] += dot3_deep(
            rth[384:512, :], rtl[384:512, :], th[384:768, cols], tl[384:768, cols]
        )
        return carry

    lax.fori_loop(0, LON // 256, adjoint_tile, 0)
    sent(3, s2, send2, 4)
    arrive(4, r2, recv2, 4)
    for u, s in ((4, 2), (5, 0), (5, 1), (5, 2)):
        transpose(1, u, s)
    sent(4, s2, send2, 4)


def finish(gf, th, tl, rth, rtl, out, rest, sem):
    w = lax.axis_index("wave")
    copies = []

    def write(src, dst, index):
        copy = pltpu.make_async_copy(src, dst, sem.at[index])
        copy.start()
        copies.append(copy)

    write(gf.at[pl.ds(0, LT)], out.at[16], 0)
    for p in range(9):
        write(gf.at[pl.ds(128 + LT * p, LT)], out.at[lax.rem(p - w + 16, 16)], 1 + p)
    rest[0:24, :] = gf[488:512, :]

    def step(n, carry):
        cols = pl.ds(pl.multiple_of(256 * n, 256), 256)
        rest[24:280, cols] = gf[512:768, cols] + dot3_deep(
            rth[512:768, :], rtl[512:768, :], th[384:768, cols], tl[384:768, cols]
        )
        for p in range(9, 16):
            pltpu.make_async_copy(
                rest.at[pl.ds(LT * (p - 9), LT), cols],
                out.at[lax.rem(p - w + 16, 16), :, cols],
                sem.at[10],
            ).start()
        return carry

    lax.fori_loop(0, LON // 256, step, 0)
    pltpu.make_async_copy(rest, rest, sem.at[10]).wait()
    for copy in copies:
        copy.wait()


def circle_table():
    wave = np.arange(DEVS * SLOTS)[:, None]
    near = 2.0 * math.pi / LON * (wave * np.arange(128)[None, :] % LON)
    far = 2.0 * math.pi / 10 * (wave * np.arange(16)[None, :] % 10)
    table = np.zeros((DEVS * SLOTS, 384))
    table[:, :128] = np.cos(near) / math.sqrt(LON)
    table[:, 128:256] = np.sin(near) / math.sqrt(LON)
    table[:, 256:272] = np.cos(far)
    table[:, 272:288] = np.sin(far)
    return table.astype(np.float32)


def level_order():
    matrix = np.zeros((LEVELS, PAD), np.float32)
    level = np.arange(LEVELS)
    matrix[level, level % LV * LEVS + level // LV] = 1
    return matrix


def local(grid_in, wavenumbers, legendre, modes_in, modes_out, damping):
    order = level_order()
    vmem = pl.BlockSpec(memory_space=pltpu.VMEM)
    hbm = pl.BlockSpec(memory_space=pl.ANY)
    dma = pltpu.SemaphoreType.DMA
    held = pl.pallas_call(
        kernel,
        out_shape=[
            pltpu.VMEM((768, LON), f32),
            pltpu.VMEM((768, LON), bf16),
            pltpu.VMEM((768, LON), bf16),
            pltpu.VMEM((768, 384), bf16),
            pltpu.VMEM((768, 384), bf16),
        ],
        in_specs=[hbm] * 9,
        out_specs=[vmem] * 5,
        scratch_shapes=[
            pltpu.VMEM((768, LON), bf16),
            pltpu.VMEM((768, LON), bf16),
            pltpu.VMEM((SLOTS * LAT, COEFF), f32),
            pltpu.VMEM((SLOTS * LAT, COEFF), bf16),
            pltpu.VMEM((SLOTS * LAT, COEFF), bf16),
            pltpu.VMEM((2 * HALF + ROWS, 128), f32),
            pltpu.VMEM((2 * HALF + ROWS, 128), f32),
            pltpu.VMEM((2 * HALF + ROWS, 128), f32),
            pltpu.VMEM((2 * HALF + ROWS, 128), f32),
            pltpu.VMEM((PAD, LAT), f32),
            pltpu.VMEM((128, LAT), f32),
            pltpu.VMEM((WAVES * 8, 128), f32),
            pltpu.VMEM((4, PAD, PAD), bf16),
            pltpu.VMEM((PAD, 1), f32),
            pltpu.VMEM((DEVS * SLOTS, 384), f32),
            pltpu.VMEM((LEVELS, LEVELS), f32),
            pltpu.VMEM((LEVELS, LEVELS), f32),
            pltpu.VMEM((LEVELS, PAD), f32),
            pltpu.VMEM((PAD, LEVELS), f32),
            pltpu.VMEM((DEVS * SLOTS + 8, 128), f32),
            pltpu.VMEM((DEVS * SLOTS + 8, 128), f32),
            pltpu.VMEM((DEVS * SLOTS + 8, 128), f32),
            pltpu.VMEM((1, DEVS * SLOTS), jnp.int32),
            pltpu.VMEM((1, LEVELS), f32),
            dma((11,)),
            dma((5,)),
            dma((5,)),
            dma((5,)),
            dma((5,)),
        ],
        compiler_params=pltpu.CompilerParams(
            collective_id=0, has_side_effects=True, vmem_limit_bytes=48 << 20
        ),
        name="spectral_step",
    )(
        wavenumbers, damping.reshape(1, -1), jnp.asarray(circle_table()),
        modes_in, modes_out, jnp.asarray(order), jnp.asarray(order.T.copy()),
        grid_in.reshape(LV, LT, LON), legendre,
    )
    result = pl.pallas_call(
        finish,
        out_shape=jax.ShapeDtypeStruct((LV, LT, LON), f32),
        in_specs=[vmem] * 5,
        out_specs=hbm,
        scratch_shapes=[
            pltpu.VMEM((280, LON), f32),
            dma((11,)),
        ],
        compiler_params=pltpu.CompilerParams(vmem_limit_bytes=40 << 20),
        name="finish",
    )(*[pltpu.with_memory_space_constraint(a, pltpu.VMEM) for a in held])
    return result.reshape(1, LV, LT, LON)


def solution(mesh):
    return jax.shard_map(
        local,
        mesh=mesh,
        in_specs=(P(None, "lev", "wave", None), P(), P(("wave", "lev"), None, None), P(), P(), P()),
        out_specs=P(None, "lev", "wave", None),
        check_vma=False,
    )
```

```python
import math

import jax
import jax.numpy as jnp
import numpy as np
from jax import lax
from jax.experimental import pallas as pl
from jax.experimental.pallas import tpu as pltpu
from jax.sharding import PartitionSpec as P

MESH = pl.DeviceIdType.MESH
f32 = jnp.float32
bf16 = jnp.bfloat16

LON = 1280
LAT = 640
COEFF = 640
WAVES = 16
LEVS = 8
DEVS = WAVES * LEVS
LV = 17
LT = 40
SLOTS = 3
LEVELS = LEVS * LV
PAD = 144
ROWS = 16
HALF = DEVS * ROWS
MAIN = 16 * LT // 128


def split(x):
    hi = x.astype(bf16)
    return hi, (x - hi.astype(f32)).astype(bf16)


def dot(a, b, dims):
    return lax.dot_general(a, b, (dims, ((), ())), preferred_element_type=f32)


TN = ((0,), (0,))
NN = ((1,), (0,))
NT = ((1,), (1,))


def dot3(ah, al, bh, bl, dims):
    rows = ah.shape[0]
    both = dot(jnp.concatenate([ah, al], 0), bh, dims)
    return both[:rows] + both[rows:] + dot(ah, bl, dims)


def dot3_deep(ah, al, bh, bl):
    return dot(jnp.concatenate([ah, al, ah], 1), jnp.concatenate([bh, bh, bl], 0), NN)


def lanes(rows):
    return lax.broadcasted_iota(jnp.int32, (rows, 128), 1)


def pick(tile, get):
    lane = lanes(8)
    value = None
    for p in range(128 * tile // LT, (128 * tile + 127) // LT + 1):
        value = get(p) if value is None else jnp.where(lane < LT * p - 128 * tile, value, get(p))
    return value


def ring(tiles, shift):
    whole, part = divmod(shift % (128 * MAIN), 128)
    if part == 0:
        return [tiles[(t + whole) % MAIN] for t in range(MAIN)]
    lane = lanes(8)
    rolled = [pltpu.roll(x, 128 - part, 1) for x in tiles]
    return [
        jnp.where(lane < 128 - part, rolled[(t + whole) % MAIN], rolled[(t + whole + 1) % MAIN])
        for t in range(MAIN)
    ]


def coordinates():
    w = lax.axis_index("wave")
    v = lax.axis_index("lev")
    return 2 * (v // 4) + w // 8, lax.rem(v, 4), lax.rem(w // 2, 4), lax.rem(w, 2)


def each_peer(visit):
    x, y, z, core = coordinates()
    xs = [lax.rem(x + a, 4) for a in range(4)]
    wave_x = [8 * lax.rem(a, 2) for a in xs]
    lev_x = [4 * (a // 2) for a in xs]
    lev_y = [lax.rem(y + b, 4) for b in range(4)]

    def outer(j, carry):
        wave_c = lax.rem(core + j // 4, 2)
        wave_z = [2 * lax.rem(z + j + d, 4) + wave_c for d in range(4)]
        for i in range(1, 16):
            a, b = i % 4, i // 4
            visit(wave_x[a] + wave_z[(b + 2 * a) % 4], lev_x[a] + lev_y[(a + b) % 4])
        return carry

    lax.fori_loop(0, 8, outer, 0)
    for j in range(1, 8):
        visit(wave_x[0] + 2 * lax.rem(z + j, 4) + lax.rem(core + j // 4, 2), lev_x[0] + lev_y[0])


def far_first():
    order = []
    for i in range(1, DEVS):
        a, b, d, core = i % 4, i // 4 % 4, i // 16 % 4, i // 64
        order.append((a, (a + b) % 4, (b + d + 2 * a) % 4, core))
    return sorted(order, key=lambda o: -sum(min(k, 4 - k) for k in o[:3]))


def each_peer_far_first(visit):
    x, y, z, core = coordinates()
    xs = [lax.rem(x + a, 4) for a in range(4)]
    wave_x = [8 * lax.rem(a, 2) for a in xs]
    lev_x = [4 * (a // 2) for a in xs]
    lev_y = [lax.rem(y + b, 4) for b in range(4)]
    wave_z = [2 * lax.rem(z + d, 4) for d in range(4)]
    wave_c = [core, 1 - core]
    for a, b, d, other in far_first():
        visit(wave_x[a] + wave_z[d] + wave_c[other], lev_x[a] + lev_y[b])


def kernel(
    waves, damp_all, circle, modes_in, modes_out, order, order_t, grid, plm,
    gf, th, tl, rth, rtl,
    gh, gl, pf, ph, pw, s1, r1, s2, r2, x, e, acc, modes, damp,
    circle_v, min_v, mout_v, order_v, order_tv, near_cos, near_sin, far, waves_row, damp_row,
    load_sem, send1, recv1, send2, recv2,
):
    w = lax.axis_index("wave")
    v = lax.axis_index("lev")
    me = w * LEVS + v

    small = [
        pltpu.make_async_copy(a, b, load_sem.at[2 + i if i < 5 else 10])
        for i, (a, b) in enumerate(
            [
                (circle, circle_v), (modes_in, min_v), (modes_out, mout_v),
                (order, order_v), (order_t, order_tv), (damp_all, damp_row),
            ]
        )
    ]
    row_copy = pltpu.make_async_copy(waves, waves_row.at[0], load_sem.at[7])
    row_copy.start()
    small[0].start()

    barrier = pltpu.get_barrier_semaphore()

    def greet(to_wave, to_lev):
        pl.semaphore_signal(barrier, inc=1, device_id=(to_wave, to_lev), device_id_type=MESH)

    each_peer(greet)
    for s in range(SLOTS):
        pltpu.make_async_copy(
            grid.at[16], gf.at[pl.ds(LT * s, LT)], load_sem.at[0]
        ).start()

    def load_level(p):
        pltpu.make_async_copy(
            grid.at[lax.rem(p - w + 16, 16)],
            gf.at[pl.ds(128 + LT * p, LT)],
            load_sem.at[0 if p < 4 else 7 + (p + 2) // 6],
        ).start()

    for p in range(4):
        load_level(p)

    for p in range(4, 16):
        load_level(p)

    slots = DEVS * SLOTS
    eye = lax.broadcasted_iota(jnp.int32, (slots, slots), 0) == lax.broadcasted_iota(
        jnp.int32, (slots, slots), 1
    )
    row_copy.wait()
    column = jnp.sum(
        jnp.where(eye, waves_row[...].astype(f32), 0.0), axis=1, keepdims=True
    ).astype(jnp.int32)
    chosen = (lax.broadcasted_iota(jnp.int32, (slots, slots), 1) == column).astype(bf16)
    small[0].wait()
    top, rest = split(circle_v[...])
    rows3 = dot(chosen, top, NN) + dot(chosen, rest, NN)
    near_cos[0:slots, :] = rows3[:, 0:128]
    near_sin[0:slots, :] = rows3[:, 128:256]
    far[0:slots, :] = rows3[:, 256:384]

    def make_table(c):
        def table(s, carry):
            mine = pl.ds(s, DEVS, SLOTS)
            rows = pl.ds(pl.multiple_of(384 * c + DEVS * s, DEVS), DEVS)
            cosine, sine, f = near_cos[mine, :], near_sin[mine, :], far[mine, :]
            first = jnp.where(c == 0, cosine, -sine)
            second = jnp.where(c == 0, sine, cosine)
            for a in range(LON // 128):
                ca, sa = f[:, a : a + 1], f[:, 16 + a : 17 + a]
                col = slice(128 * a, 128 * a + 128)
                th[rows, col], tl[rows, col] = split(first * ca - second * sa)
            return carry

        lax.fori_loop(0, SLOTS, table, 0)

    def loaded(rows, index):
        part = gf.at[pl.ds(0, rows)]
        pltpu.make_async_copy(part, part, load_sem.at[index]).wait()

    def split_grid(i, carry):
        rows = pl.ds(pl.multiple_of(32 * i, 32), 32)
        gh[rows, :], gl[rows, :] = split(gf[rows, :])
        return carry

    lane128 = lanes(128)

    def forward_dft(c, n):
        cols = pl.ds(pl.multiple_of(256 * n, 256), 256)
        part = pl.ds(pl.multiple_of(384 * c, 128), 384)
        y = dot3(th[part, :], tl[part, :], gh[cols, :], gl[cols, :], NT)
        y0, y1 = y[:, 0:128], y[:, 128:256]

        @pl.when(n == 0)
        def _():
            last = jnp.where(
                lane128 < LT, y0[0:128], jnp.where(lane128 < 2 * LT, y0[128:256], y0[256:384])
            )
            s1[pl.ds(HALF * c, DEVS, ROWS), :] = last

        @pl.when(n > 0)
        def _():
            for s in range(SLOTS):
                s1[pl.ds(HALF * c + 6 * n - 2 + s, DEVS, ROWS), :] = y0[128 * s : 128 * s + 128]

        for s in range(SLOTS):
            s1[pl.ds(HALF * c + 6 * n + 1 + s, DEVS, ROWS), :] = y1[128 * s : 128 * s + 128]

    def send(c, h, src, dst, send_sem, recv_sem):
        send_rows(each_peer, c, 8 * h, 8, 2 * c + h, src, dst, send_sem, recv_sem)

    def send_rows(each, c, first, rows, index, src, dst, send_sem, recv_sem):

        def block(d):
            return pl.ds(pl.multiple_of((c * DEVS + d) * ROWS + first, rows), rows)

        pltpu.make_async_copy(src.at[block(me)], dst.at[block(me)], recv_sem.at[index]).start()

        def go(to_wave, to_lev):
            pltpu.make_async_remote_copy(
                src_ref=src.at[block(to_wave * LEVS + to_lev)],
                dst_ref=dst.at[block(me)],
                send_sem=send_sem.at[index],
                recv_sem=recv_sem.at[index],
                device_id=(to_wave, to_lev),
                device_id_type=MESH,
            ).start()

        each(go)

    def arrive(index, dst, recv_sem, rows=8):
        part = dst.at[pl.ds(0, DEVS * rows)]
        pltpu.make_async_copy(part, part, recv_sem.at[index]).wait()

    def sent(index, src, send_sem, rows=8):
        part = src.at[pl.ds(0, (DEVS - 1) * rows)]
        pltpu.make_async_copy(part, part, send_sem.at[index]).wait()

    def forward(i, carry):
        c, n = i // 3, lax.rem(i, 3)

        @pl.when(n == 0)
        def _():
            make_table(c)

        @pl.when(i == 0)
        def _():
            loaded(7 * LT, 0)
            gf[120:128, :] = jnp.zeros((8, LON), f32)

        @pl.when((i == 1) | (i == 2))
        def _():
            loaded(6 * LT, 7 + i)

        @pl.when(i == 2)
        def _():
            for copy in small[1:]:
                copy.start()
            for s in range(SLOTS):
                pltpu.make_async_copy(
                    plm.at[s], pf.at[pl.ds(LAT * s, LAT)], load_sem.at[1]
                ).start()

        @pl.when(c == 0)
        def _():
            lax.fori_loop(8 * n, 8 * n + 8, split_grid, 0)

        forward_dft(c, n)

        @pl.when(i == 0)
        def _():
            pl.semaphore_wait(barrier, DEVS - 1)

        @pl.when(i < 2)
        def _():
            send_rows(each_peer, 0, 4 * i, 4, 4 * i, s1, r1, send1, recv1)

        @pl.when((n > 0) & (i != 1))
        def _():
            send(c, n - 1, s1, r1, send1, recv1)

        return carry

    lax.fori_loop(0, 6, forward, 0)

    pltpu.make_async_copy(pf, pf, load_sem.at[1]).wait()

    def split_plm(i, carry):
        rows = pl.ds(pl.multiple_of(64 * i, 64), 64)
        ph[rows, :], pw[rows, :] = split(pf[rows, :])
        return carry

    lax.fori_loop(0, SLOTS * LAT // 64, split_plm, 0)

    for copy in small[1:]:
        copy.wait()
    pad = PAD - LEVELS
    for i, part in enumerate(split(jnp.concatenate([min_v[...], jnp.zeros((pad, LEVELS), f32)], 0))):
        modes[i] = dot(part, order_v[...].astype(bf16), NN).astype(bf16)
    for i, part in enumerate(split(jnp.concatenate([mout_v[...], jnp.zeros((LEVELS, pad), f32)], 1))):
        modes[2 + i] = dot(order_tv[...].astype(bf16), part, NN).astype(bf16)
    eye = lax.broadcasted_iota(jnp.int32, (PAD, LEVELS), 0) == lax.broadcasted_iota(
        jnp.int32, (PAD, LEVELS), 1
    )
    damp[...] = jnp.sum(jnp.where(eye, damp_row[...], 0.0), axis=1, keepdims=True)
    x[LEVELS:PAD, :] = jnp.zeros((PAD - LEVELS, LAT), f32)
    lane8 = lanes(8)

    def middle(c, outer):
        @pl.when(c == 0)
        def _():
            arrive(0, r1, recv1, 4)
            arrive(4, r1, recv1, 4)

        @pl.when(c == 1)
        def _():
            arrive(2, r1, recv1)

        arrive(2 * c + 1, r1, recv1)
        acc[...] = jnp.zeros((WAVES * 8, 128), f32)

        def slot(s, carry):
            base = HALF * c + 1 + s
            for k in range(16):
                tiles = [
                    pick(t, lambda p: r1[pl.ds(base + ((p - k) % 16) * 128 + 3 * t, 8, ROWS), :])
                    for t in range(MAIN)
                ]
                for t, value in enumerate(ring(tiles, LT * k)):
                    x[8 * k : 8 * k + 8, 128 * t : 128 * t + 128] = value
            tiles = [None] * MAIN
            for q in range(WAVES):
                own = r1[pl.ds(HALF * c + q * 128, 8, ROWS), :]
                own = pltpu.roll(own, lax.rem(LT * q - LT * s + 768, 128), 1)
                t, off = divmod(LT * q, 128)
                tiles[t] = own if off == 0 else jnp.where(lane8 < off, tiles[t], own)
                if off + LT > 128:
                    tiles[t + 1] = own
            for t in range(MAIN):
                x[128:136, 128 * t : 128 * t + 128] = tiles[t]

            prow = pl.ds(pl.multiple_of(LAT * s, LAT), LAT)
            xh, xl = split(x[...])
            spec = dot3(xh, xl, ph[prow, :], pw[prow, :], NN)
            here = lax.broadcasted_iota(jnp.int32, (1, slots), 1) == SLOTS * me + s
            wave = jnp.sum(
                jnp.where(here, waves_row[...].astype(f32), 0.0), axis=1, keepdims=True
            ).astype(jnp.int32)
            degree = wave + lax.broadcasted_iota(jnp.int32, (PAD, COEFF), 1)
            growth = (degree * (degree + 1)).astype(f32)
            factor = jnp.where(degree < COEFF, 1.0 / (1.0 + damp[...] * growth), 0.0)
            sh, sl = split(spec)
            modal = dot3(modes[0], modes[1], sh, sl, NN) * factor
            mh, ml = split(modal)
            solved = dot3(modes[2], modes[3], mh, ml, NN)
            vh, vl = split(solved)
            x[...] = dot3(vh, vl, ph[prow, :], pw[prow, :], NT)

            for k in range(16):
                tiles = [x[8 * k : 8 * k + 8, 128 * t : 128 * t + 128] for t in range(MAIN)]
                for t, value in enumerate(ring(tiles, -LT * k)):
                    e[8 * k : 8 * k + 8, 128 * t : 128 * t + 128] = value
            for q in range(WAVES):
                for t in range(MAIN):

                    def get(p):
                        k = (p - q) % 16
                        return e[8 * k : 8 * k + 8, 128 * t : 128 * t + 128]

                    s2[pl.ds(base + q * 128 + 3 * t, 8, ROWS), :] = pick(t, get)
                t, off = divmod(LT * q, 128)
                own = x[128:136, 128 * t : 128 * t + 128]
                if off + LT > 128:
                    after = x[128:136, 128 * t + 128 : 128 * t + 256]
                    own = jnp.where(lane8 < off, after, own)
                own = pltpu.roll(own, lax.rem(LT * s - LT * q + 768, 128), 1)
                inside = (lane8 >= LT * s) & (lane8 < LT * s + LT)
                acc[8 * q : 8 * q + 8, :] = jnp.where(inside, own, acc[8 * q : 8 * q + 8, :])
            return carry

        lax.fori_loop(0, SLOTS, slot, 0)
        s2[pl.ds(HALF * c, DEVS, ROWS), :] = acc[...]


        def out_half(h, carry):
            @pl.when((c == 0) | (h == 0))
            def _():
                send_rows(
                    each_peer_far_first, c, 8 * h, 8, 2 * c + h, s2, r2, send2, recv2
                )

            @pl.when((c == 1) & (h > 0))
            def _():
                send_rows(
                    each_peer_far_first, c, 4 + 4 * h, 4, 2 + h, s2, r2, send2, recv2
                )

            return carry

        lax.fori_loop(0, 2 + c, out_half, 0)
        return outer

    lax.fori_loop(0, 2, middle, 0)

    def transpose(c, u, s):
        start = jnp.where(u == 0, 0, 3 * u - 2 + s)
        tile = r2[pl.ds(HALF * c + start, DEVS, ROWS), :]
        inside = (lane128 >= LT * s) & (lane128 < LT * s + LT)
        tile = jnp.where(inside | (u > 0), tile, 0.0)
        rows_u = pl.ds(pl.multiple_of(128 * u, 128), 128)
        cols_s = slice(128 * s, 128 * s + 128)
        rth[rows_u, cols_s], rtl[rows_u, cols_s] = split(tile.T)

    def returned(j, carry):
        c, h = j // 2, lax.rem(j, 2)
        rows = pl.ds(pl.multiple_of(384 * h, 128), 384)
        part = pl.ds(pl.multiple_of(384 * c, 128), 384)
        arrive(j, r2, recv2)
        for i in range(3):
            for s in range(SLOTS):
                transpose(c, 3 * h + i, s)

        def adjoint(n, inner):
            cols = pl.ds(pl.multiple_of(256 * n, 256), 256)
            y = dot3_deep(rth[rows, :], rtl[rows, :], th[part, cols], tl[part, cols])
            gf[rows, cols] = jnp.where(c == 0, y, gf[rows, cols] + y)
            return inner

        lax.fori_loop(0, LON // 256, adjoint, 0)
        return carry

    lax.fori_loop(0, 3, returned, 0)
    gf[0:40, :] = gf[0:40, :] + gf[40:80, :] + gf[80:120, :]
    for index in range(1, 4):
        sent(index, s1, send1)
    sent(0, s1, send1, 4)
    sent(4, s1, send1, 4)
    for index in range(3):
        sent(index, s2, send2)
    arrive(3, r2, recv2, 4)
    for u, s in ((3, 0), (3, 1), (3, 2), (4, 0), (4, 1)):
        transpose(1, u, s)

    def adjoint_tile(n, carry):
        cols = pl.ds(pl.multiple_of(256 * n, 256), 256)
        gf[384:512, cols] += dot3_deep(
            rth[384:512, :], rtl[384:512, :], th[384:768, cols], tl[384:768, cols]
        )
        return carry

    lax.fori_loop(0, LON // 256, adjoint_tile, 0)
    sent(3, s2, send2, 4)
    arrive(4, r2, recv2, 4)
    for u, s in ((4, 2), (5, 0), (5, 1), (5, 2)):
        transpose(1, u, s)
    sent(4, s2, send2, 4)


def finish(gf, th, tl, rth, rtl, out, rest, sem):
    w = lax.axis_index("wave")
    copies = []

    def write(src, dst, index):
        copy = pltpu.make_async_copy(src, dst, sem.at[index])
        copy.start()
        copies.append(copy)

    write(gf.at[pl.ds(0, LT)], out.at[16], 0)
    for p in range(9):
        write(gf.at[pl.ds(128 + LT * p, LT)], out.at[lax.rem(p - w + 16, 16)], 1 + p)
    rest[0:24, :] = gf[488:512, :]

    def step(n, carry):
        cols = pl.ds(pl.multiple_of(256 * n, 256), 256)
        rest[24:280, cols] = gf[512:768, cols] + dot3_deep(
            rth[512:768, :], rtl[512:768, :], th[384:768, cols], tl[384:768, cols]
        )
        for p in range(9, 16):
            pltpu.make_async_copy(
                rest.at[pl.ds(LT * (p - 9), LT), cols],
                out.at[lax.rem(p - w + 16, 16), :, cols],
                sem.at[10],
            ).start()
        return carry

    lax.fori_loop(0, LON // 256, step, 0)
    pltpu.make_async_copy(rest, rest, sem.at[10]).wait()
    for copy in copies:
        copy.wait()


def circle_table():
    wave = np.arange(DEVS * SLOTS)[:, None]
    near = 2.0 * math.pi / LON * (wave * np.arange(128)[None, :] % LON)
    far = 2.0 * math.pi / 10 * (wave * np.arange(16)[None, :] % 10)
    table = np.zeros((DEVS * SLOTS, 384))
    table[:, :128] = np.cos(near) / math.sqrt(LON)
    table[:, 128:256] = np.sin(near) / math.sqrt(LON)
    table[:, 256:272] = np.cos(far)
    table[:, 272:288] = np.sin(far)
    return table.astype(np.float32)


def level_order():
    matrix = np.zeros((LEVELS, PAD), np.float32)
    level = np.arange(LEVELS)
    matrix[level, level % LV * LEVS + level // LV] = 1
    return matrix


def local(grid_in, wavenumbers, legendre, modes_in, modes_out, damping):
    order = level_order()
    vmem = pl.BlockSpec(memory_space=pltpu.VMEM)
    hbm = pl.BlockSpec(memory_space=pl.ANY)
    dma = pltpu.SemaphoreType.DMA
    held = pl.pallas_call(
        kernel,
        out_shape=[
            pltpu.VMEM((768, LON), f32),
            pltpu.VMEM((768, LON), bf16),
            pltpu.VMEM((768, LON), bf16),
            pltpu.VMEM((768, 384), bf16),
            pltpu.VMEM((768, 384), bf16),
        ],
        in_specs=[hbm] * 9,
        out_specs=[vmem] * 5,
        scratch_shapes=[
            pltpu.VMEM((768, LON), bf16),
            pltpu.VMEM((768, LON), bf16),
            pltpu.VMEM((SLOTS * LAT, COEFF), f32),
            pltpu.VMEM((SLOTS * LAT, COEFF), bf16),
            pltpu.VMEM((SLOTS * LAT, COEFF), bf16),
            pltpu.VMEM((2 * HALF + ROWS, 128), f32),
            pltpu.VMEM((2 * HALF + ROWS, 128), f32),
            pltpu.VMEM((2 * HALF + ROWS, 128), f32),
            pltpu.VMEM((2 * HALF + ROWS, 128), f32),
            pltpu.VMEM((PAD, LAT), f32),
            pltpu.VMEM((128, LAT), f32),
            pltpu.VMEM((WAVES * 8, 128), f32),
            pltpu.VMEM((4, PAD, PAD), bf16),
            pltpu.VMEM((PAD, 1), f32),
            pltpu.VMEM((DEVS * SLOTS, 384), f32),
            pltpu.VMEM((LEVELS, LEVELS), f32),
            pltpu.VMEM((LEVELS, LEVELS), f32),
            pltpu.VMEM((LEVELS, PAD), f32),
            pltpu.VMEM((PAD, LEVELS), f32),
            pltpu.VMEM((DEVS * SLOTS + 8, 128), f32),
            pltpu.VMEM((DEVS * SLOTS + 8, 128), f32),
            pltpu.VMEM((DEVS * SLOTS + 8, 128), f32),
            pltpu.VMEM((1, DEVS * SLOTS), jnp.int32),
            pltpu.VMEM((1, LEVELS), f32),
            dma((11,)),
            dma((5,)),
            dma((5,)),
            dma((5,)),
            dma((5,)),
        ],
        compiler_params=pltpu.CompilerParams(
            collective_id=0, has_side_effects=True, vmem_limit_bytes=48 << 20
        ),
        name="spectral_step",
    )(
        wavenumbers, damping.reshape(1, -1), jnp.asarray(circle_table()),
        modes_in, modes_out, jnp.asarray(order), jnp.asarray(order.T.copy()),
        grid_in.reshape(LV, LT, LON), legendre,
    )
    result = pl.pallas_call(
        finish,
        out_shape=jax.ShapeDtypeStruct((LV, LT, LON), f32),
        in_specs=[vmem] * 5,
        out_specs=hbm,
        scratch_shapes=[
            pltpu.VMEM((280, LON), f32),
            dma((11,)),
        ],
        compiler_params=pltpu.CompilerParams(vmem_limit_bytes=40 << 20),
        name="finish",
    )(*[pltpu.with_memory_space_constraint(a, pltpu.VMEM) for a in held])
    return result.reshape(1, LV, LT, LON)


def solution(mesh):
    return jax.shard_map(
        local,
        mesh=mesh,
        in_specs=(P(None, "lev", "wave", None), P(), P(("wave", "lev"), None, None), P(), P(), P()),
        out_specs=P(None, "lev", "wave", None),
        check_vma=False,
    )
```
